32 devices in a mesh: region: 8 (over z, x), member: 4 (over y, core).
Axes of the slice: x: 2, y: 2, z: 4, core: 2. Of those that a mesh axis runs over, the one named last changes fastest.
Arguments:
- ensemble: bfloat16 [128, 16, 64, 512], P('region', 'member'), may hold values from -6 to 6
- increment: bfloat16 [128, 64, 512], P('region'), may hold values from -6 to 6
- coords: bfloat16 [128, 2, 512], P('region'), may hold values from -4.5 to 5.5
- sent_slots: int32 [8, 8, 1], P('region'), may hold values from 0 to 15, as said below
- pair_list: int32 [128, 2], P('region'), may hold values from 0 to 7, as said below
- pair_count: int32 [8], P('region'), may hold values from 8 to 16, as said below
Outputs:
- covariance_product: float32 [128, 64, 512], P('region', 'member')
The draws below stay inside these ranges and needn't reach their ends.
Inputs may be any that keep to these rules, and one draw needn't show every extreme that they name: `sent_slots`: the k numbers of one home and owner are distinct. `pair_list`: the two slots of a row differ; every received slot is named by some live row of its owner. `pair_count`: some owner has exactly 16 live pairs and some has 8.
All inputs are finite; a program needn't handle non-finite values.
Results may differ from the reference program's by a relative error of at most 0.0028.
Values may be sent and summed in bfloat16 or wider, within the bound.
A program may use at most 128 MiB of HBM per device.

```python
import jax
import jax.numpy as jnp
from jax import lax

PTS = 512
LEV = 64
BLK_DEV = 16
REQ = 1
NB = 128
MEMBERS = 16
PAIR_CAP = 16
N_REGION = 8


def draw_coords(key, part):
    first_key, second_key = jax.random.split(key, 2)
    centre = jax.random.uniform(first_key, (NB, 2, 1), jnp.float32, 0.0, 1.0)
    offset = jax.random.uniform(second_key, (NB, 2, PTS), jnp.float32, -4.0, 4.0)
    return (centre + offset).astype(jnp.bfloat16)


def draw_sent_slots(key, part):
    scores = jax.random.randint(key, (N_REGION, N_REGION, BLK_DEV), 0, 1 << 20) * BLK_DEV + jnp.arange(BLK_DEV, dtype=jnp.int32)
    ranked = jnp.argsort(scores, axis=-1)
    return ranked[:, :, :REQ].astype(jnp.int32)


def draw_pair_list(key, part):
    slot_total = N_REGION * REQ
    first_key, second_key, third_key = jax.random.split(key, 3)
    scores = jax.random.randint(first_key, (N_REGION, slot_total), 0, 1 << 20) * slot_total + jnp.arange(slot_total, dtype=jnp.int32)
    ranked = jnp.argsort(scores, axis=-1).astype(jnp.int32)
    cycle_second = jnp.roll(ranked, -1, axis=1)
    extra_first = jax.random.randint(second_key, (N_REGION, slot_total), 0, slot_total)
    extra_second = (extra_first + jax.random.randint(third_key, (N_REGION, slot_total), 1, slot_total)) % slot_total
    first_slot = jnp.concatenate([ranked, extra_first], axis=1)
    second_slot = jnp.concatenate([cycle_second, extra_second], axis=1)
    return jnp.stack([first_slot, second_slot], axis=-1).reshape(N_REGION * 2 * slot_total, 2).astype(jnp.int32)


def draw_pair_count(key, part):
    slot_total = N_REGION * REQ
    first_key, second_key, third_key = jax.random.split(key, 3)
    counts = jax.random.randint(first_key, (N_REGION,), slot_total, 2 * slot_total + 1)
    busiest = jax.random.randint(second_key, (), 0, N_REGION)
    lightest = (busiest + jax.random.randint(third_key, (), 1, N_REGION)) % N_REGION
    owners = jnp.arange(N_REGION, dtype=jnp.int32)
    counts = jnp.where(owners == busiest, 2 * slot_total, jnp.where(owners == lightest, slot_total, counts))
    return counts.astype(jnp.int32)


def block_scale(own_key, shape, cuts, least, high):
    loudness, own = 1.0, jax.random.fold_in(own_key, 6)
    for dim, shards_of in cuts:
        draws = jnp.exp(jax.random.uniform(jax.random.fold_in(own, dim), (shards_of,), jnp.float32, least / len(cuts), high / len(cuts)))
        loudness = loudness * jnp.repeat(draws, shape[dim] // shards_of).reshape([-1 if axis == dim else 1 for axis in range(len(shape))])
    return loudness


def scatter_about(own_key, extent, spread, limit, pieces=(), kind=jnp.bfloat16):
    entries = jax.random.normal(own_key, extent, jnp.float32) * spread
    if len(pieces) > 0:
        entries = block_scale(own_key, extent, pieces, -0.22, 0.18) * entries
    return jnp.clip(entries, min=-limit, max=limit).astype(kind)


def setup_inputs(seed: int = 0) -> dict:
    keys = jax.random.split(jax.random.key(seed), 7)
    ensemble = scatter_about(keys[0], (NB, MEMBERS, LEV, PTS), 1.0, 6.0, ((0, 8), (1, 4)))
    increment = scatter_about(keys[1], (NB, LEV, PTS), 1.0, 6.0, ((0, 8),))
    coords = draw_coords(jax.random.fold_in(keys[6], 71), 0)
    sent_slots = draw_sent_slots(jax.random.fold_in(keys[6], 71), 0)
    pair_list = draw_pair_list(jax.random.fold_in(keys[6], 71), 0)
    pair_count = draw_pair_count(jax.random.fold_in(keys[6], 71), 0)
    return dict(ensemble=ensemble, increment=increment, coords=coords, sent_slots=sent_slots, pair_list=pair_list, pair_count=pair_count)


def gaspari_cohn(distance):
    inside_part = (((-0.25 * distance + 0.5) * distance + 0.625) * distance - 5.0 / 3.0) * distance * distance + 1.0
    floored = jnp.maximum(distance, 1.0)
    outside_part = ((((distance / 12.0 - 0.5) * distance + 0.625) * distance + 5.0 / 3.0) * distance - 5.0) * distance + 4.0 - 2.0 / (3.0 * floored)
    return jnp.where(distance <= 1.0, inside_part, jnp.where(distance < 2.0, outside_part, 0.0))

def tile_of(left_where, right_where):
    left_float = left_where.astype(jnp.float32)
    right_float = right_where.astype(jnp.float32)
    east_gap = left_float[0][:, None] - right_float[0][None, :]
    north_gap = left_float[1][:, None] - right_float[1][None, :]
    return gaspari_cohn(jnp.sqrt(east_gap * east_gap + north_gap * north_gap)).astype(jnp.bfloat16)

def reference(ensemble, increment, coords, sent_slots, pair_list, pair_count):
    blocks, members, levels, points = ensemble.shape
    weighted = (ensemble.astype(jnp.float32) * increment[:, None].astype(jnp.float32)).astype(jnp.bfloat16)
    flat_blocks = weighted.reshape(blocks, members * levels, points)

    def diag_one(pair_entry):
        member_rows, places = pair_entry
        local_tile = tile_of(places, places)
        return lax.dot_general(member_rows, local_tile, (((1,), (1,)), ((), ())), preferred_element_type=jnp.float32)
    field_sum = lax.map(diag_one, (flat_blocks, coords))
    homes = jnp.arange(N_REGION, dtype=jnp.int32)
    block_table = homes[:, None, None] * BLK_DEV + sent_slots
    block_table = jnp.transpose(block_table, (1, 0, 2)).reshape(N_REGION, N_REGION * REQ)
    owner_of = jnp.repeat(jnp.arange(N_REGION, dtype=jnp.int32), PAIR_CAP)
    row_index = jnp.tile(jnp.arange(PAIR_CAP, dtype=jnp.int32), N_REGION)
    live_flags = row_index < pair_count[owner_of]
    first_block = block_table[owner_of, pair_list[:, 0]]
    second_block = block_table[owner_of, pair_list[:, 1]]

    def add_pair(totals, pair_entry):
        first_one, second_one, is_live = pair_entry

        def apply_pair(current):
            local_tile = tile_of(coords[first_one], coords[second_one])
            to_first = lax.dot_general(flat_blocks[second_one], local_tile, (((1,), (1,)), ((), ())), preferred_element_type=jnp.float32)
            to_second = jnp.dot(flat_blocks[first_one], local_tile, preferred_element_type=jnp.float32)
            current = current.at[first_one].add(to_first)
            return current.at[second_one].add(to_second)
        return (lax.cond(is_live, apply_pair, lambda current: current, totals), None)
    field_sum, _ = lax.scan(add_pair, field_sum, (first_block, second_block, live_flags))
    combined = lax.optimization_barrier(jnp.sum(ensemble.astype(jnp.float32) * field_sum.reshape(blocks, members, levels, points), axis=1))
    return combined / (members - 1)
```

```python
import functools

import jax
import jax.numpy as jnp
from jax import lax
from jax.experimental import pallas as pl
from jax.experimental.pallas import tpu as pltpu
from jax.sharding import PartitionSpec as P

MESH = pl.DeviceIdType.MESH
ROWS = 32
TILE_BYTES = 24 << 20


def left_right(where):
    east, north = where[0:1], where[1:2]
    norm = east * east + north * north
    high = norm.astype(jnp.bfloat16).astype(jnp.float32)
    middle = (norm - high).astype(jnp.bfloat16).astype(jnp.float32)
    low = norm - high - middle
    row = lax.broadcasted_iota(jnp.int32, (16, where.shape[1]), 0)

    def stack(entries):
        out = jnp.zeros(row.shape, jnp.float32)
        for k, entry in enumerate(entries):
            out = jnp.where(row == k, entry, out)
        return out.astype(jnp.bfloat16)

    return (
        stack([east, north, high, middle, low, 1.0, 1.0, 1.0]),
        stack([-2.0 * east, -2.0 * north, 1.0, 1.0, 1.0, high, middle, low]),
    )


def gaspari_cohn(square):
    square = jnp.maximum(square, 2.0**-10)
    inverse = lax.rsqrt(square)
    z = square * inverse
    far = jnp.maximum(2.0 - z, 0.0)
    near = jnp.maximum(1.0 - z, 0.0)
    far = far * far
    near = near * near
    near = near + near
    both = square + z
    total = (far * far) * (both + (z - 0.5)) + (near * near) * (2.0 - both)
    return (total * (inverse * (1.0 / 12.0))).astype(jnp.bfloat16)


def kernel(
    regions, groups, levels,
    slots_ref, many_ref, ens_ref, inc_ref, where_ref,
    out_ref,
    place_out, place_in, rows_out, rows_in, weights, field, tiles, square, diag_part, diag_in,
    pair_part, pair_in, home_out, home_in,
    place_send, place_recv, rows_send, rows_recv, diag_send, diag_recv, pair_send, pair_recv,
    home_send, home_recv,
):
    blocks, rows, points = ens_ref.shape
    members = rows // levels
    share = levels // groups
    me = lax.axis_index("region")
    my_group = lax.axis_index("member")

    def to_region(src, dst, send, recv, d):
        return pltpu.make_async_remote_copy(
            src_ref=src.at[d], dst_ref=dst.at[d], send_sem=send.at[d], recv_sem=recv.at[d],
            device_id=(lax.rem(me + d, regions), my_group), device_id_type=MESH,
        )

    def back_to_region(src, dst, send, recv, d):
        return pltpu.make_async_remote_copy(
            src_ref=src.at[d], dst_ref=dst.at[d], send_sem=send.at[d], recv_sem=recv.at[d],
            device_id=(lax.rem(me + regions - d, regions), my_group), device_id_type=MESH,
        )

    def to_group(src, dst, send, recv, d):
        other = lax.rem(my_group + d, groups)
        return pltpu.make_async_remote_copy(
            src_ref=src.at[other], dst_ref=dst.at[d], send_sem=send.at[d], recv_sem=recv.at[d],
            device_id=(me, other), device_id_type=MESH,
        )

    barrier = pltpu.get_barrier_semaphore()

    @pl.loop(1, regions)
    def _(d):
        pl.semaphore_signal(
            barrier, inc=1, device_id=(lax.rem(me + d, regions), my_group), device_id_type=MESH
        )

    @pl.loop(1, groups)
    def _(d):
        pl.semaphore_signal(
            barrier, inc=1, device_id=(me, lax.rem(my_group + d, groups)), device_id_type=MESH
        )

    for d in range(regions):
        slot = slots_ref[lax.rem(me + d, regions)]
        places, sent = (place_in, rows_in) if d == 0 else (place_out, rows_out)
        places[d] = where_ref[slot]
        sent[d, 0:rows] = ens_ref[slot]
        sent[d, rows : rows + levels] = inc_ref[slot]
    pl.semaphore_wait(barrier, regions + groups - 2)

    @pl.loop(1, regions)
    def _(d):
        to_region(place_out, place_in, place_send, place_recv, d).start()

    @pl.loop(1, regions)
    def _(d):
        to_region(rows_out, rows_in, rows_send, rows_recv, d).start()

    def weigh(member_rows, factor):
        factor = factor.astype(jnp.float32)
        return jnp.concatenate(
            [
                (member_rows[m * levels : (m + 1) * levels].astype(jnp.float32) * factor).astype(
                    jnp.bfloat16
                )
                for m in range(members)
            ],
            0,
        )

    def over_members(member_rows, results):
        total = None
        for m in range(members):
            cut = slice(m * levels, (m + 1) * levels)
            term = member_rows[cut].astype(jnp.float32) * results[cut]
            total = term if total is None else total + term
        return total

    def make_tile(index, left_where, right_where):
        left, _ = left_right(left_where)
        _, right = left_right(right_where)
        square[...] = lax.dot_general(
            left, right, (((0,), (0,)), ((), ())), preferred_element_type=jnp.float32
        )

        @pl.loop(0, points // ROWS)
        def _(step):
            cut = pl.ds(pl.multiple_of(step * ROWS, ROWS), ROWS)
            tiles[index, cut] = gaspari_cohn(square[cut])

    @pl.loop(0, blocks)
    def _(b):
        make_tile(0, where_ref[b], where_ref[b])
        member_rows = ens_ref[b]
        results = jnp.dot(
            weigh(member_rows, inc_ref[b]), tiles[0], preferred_element_type=jnp.float32
        )
        total = over_members(member_rows, results)
        for g in range(groups):
            diag_part[g, b] = total[g * share : (g + 1) * share]

    @pl.loop(1, groups)
    def _(d):
        to_group(diag_part, diag_in, diag_send, diag_recv, d).start()

    @pl.loop(1, regions)
    def _(d):
        to_region(place_out, place_in, place_send, place_recv, d).wait()

    keep = tiles.shape[0] > 1
    if keep:

        @pl.loop(1, regions)
        def _(v):
            @pl.loop(0, v)
            def _(u):
                make_tile(v * (v - 1) // 2 + u, place_in[u], place_in[v])

    field[...] = jnp.zeros_like(field)
    weights[0] = weigh(rows_in[0, 0:rows], rows_in[0, rows : rows + levels])

    @pl.loop(1, regions)
    def _(v):
        to_region(rows_out, rows_in, rows_send, rows_recv, v).wait()
        weights[v] = weigh(rows_in[v, 0:rows], rows_in[v, rows : rows + levels])
        second = lax.rem(me + regions - v, regions)

        @pl.loop(0, v)
        def _(u):
            first = lax.rem(me + regions - u, regions)
            times = many_ref[first * regions + second]
            index = v * (v - 1) // 2 + u if keep else 0
            if not keep:
                make_tile(0, place_in[u], place_in[v])
            field[u] += times * lax.dot_general(
                weights[v], tiles[index], (((1,), (1,)), ((), ())),
                preferred_element_type=jnp.float32,
            )
            field[v] += times * jnp.dot(
                weights[u], tiles[index], preferred_element_type=jnp.float32
            )

    @pl.loop(0, regions)
    def _(d):
        total = over_members(rows_in[d, 0:rows], field[d]).astype(pair_part.dtype)
        for g in range(groups):
            pair_part[g, d] = total[g * share : (g + 1) * share]

    @pl.loop(1, groups)
    def _(d):
        to_group(pair_part, pair_in, pair_send, pair_recv, d).start()

    @pl.loop(1, groups)
    def _(d):
        to_group(diag_part, diag_in, diag_send, diag_recv, d).wait()

    @pl.loop(1, groups)
    def _(d):
        to_group(pair_part, pair_in, pair_send, pair_recv, d).wait()

    for d in range(regions):
        total = pair_part[my_group, d].astype(jnp.float32)
        for g in range(1, groups):
            total = total + pair_in[g, d].astype(jnp.float32)
        (home_in if d == 0 else home_out)[d] = total

    @pl.loop(1, regions)
    def _(d):
        back_to_region(home_out, home_in, home_send, home_recv, d).start()

    @pl.loop(0, blocks)
    def _(b):
        total = diag_part[my_group, b]
        for g in range(1, groups):
            total = total + diag_in[g, b]
        out_ref[b] = total

    @pl.loop(1, regions)
    def _(d):
        back_to_region(home_out, home_in, home_send, home_recv, d).wait()

    @pl.loop(0, blocks)
    def _(b):
        total = out_ref[b]
        for d in range(regions):
            here = jnp.where(slots_ref[lax.rem(me + d, regions)] == b, 1.0, 0.0)
            total = total + here * home_in[d]
        out_ref[b] = total


def per_device(ensemble, increment, coords, sent_slots, pair_list, pair_count):
    blocks, members, levels, points = ensemble.shape
    regions, groups = lax.axis_size("region"), lax.axis_size("member")
    share = levels // groups
    rows = members * levels
    live = jnp.arange(pair_list.shape[0], dtype=jnp.int32) < pair_count[0]
    low = jnp.min(pair_list, axis=1)
    high = jnp.max(pair_list, axis=1)
    home = jnp.arange(regions, dtype=jnp.int32)
    first, second = home[:, None, None], home[None, :, None]
    hit = (jnp.minimum(first, second) == low) & (jnp.maximum(first, second) == high) & live
    many = jnp.sum(hit.astype(jnp.float32), axis=2).reshape(regions * regions)
    where = jnp.pad(coords.astype(jnp.float32), ((0, 0), (0, 6), (0, 0)))
    pairs = regions * (regions - 1) // 2
    tile_total = pairs if pairs * points * points * 2 <= TILE_BYTES else 1
    part_kind = jnp.bfloat16 if share % 16 == 0 else jnp.float32
    vmem, smem = pl.BlockSpec(memory_space=pltpu.VMEM), pl.BlockSpec(memory_space=pltpu.SMEM)
    region_dma = pltpu.SemaphoreType.DMA((regions,))
    group_dma = pltpu.SemaphoreType.DMA((groups,))
    f32, bf16 = jnp.float32, jnp.bfloat16
    summed = pl.pallas_call(
        functools.partial(kernel, regions, groups, levels),
        out_shape=jax.ShapeDtypeStruct((blocks, share, points), f32),
        in_specs=[smem, smem, vmem, vmem, vmem],
        out_specs=vmem,
        scratch_shapes=[
            pltpu.VMEM((regions, 8, points), f32),
            pltpu.VMEM((regions, 8, points), f32),
            pltpu.VMEM((regions, rows + levels, points), bf16),
            pltpu.VMEM((regions, rows + levels, points), bf16),
            pltpu.VMEM((regions, rows, points), bf16),
            pltpu.VMEM((regions, rows, points), f32),
            pltpu.VMEM((tile_total, points, points), bf16),
            pltpu.VMEM((points, points), f32),
            pltpu.VMEM((groups, blocks, share, points), f32),
            pltpu.VMEM((groups, blocks, share, points), f32),
            pltpu.VMEM((groups, regions, share, points), part_kind),
            pltpu.VMEM((groups, regions, share, points), part_kind),
            pltpu.VMEM((regions, share, points), f32),
            pltpu.VMEM((regions, share, points), f32),
        ]
        + [region_dma] * 4 + [group_dma] * 4 + [region_dma] * 2,
        compiler_params=pltpu.CompilerParams(
            collective_id=0, has_side_effects=True, vmem_limit_bytes=56 << 20
        ),
    )(
        sent_slots[0, :, 0],
        many,
        ensemble.reshape(blocks, rows, points),
        increment,
        where,
    )
    return summed / (members * groups - 1)


def solution(mesh):
    in_specs = (
        P("region", "member", None, None),
        P("region", None, None),
        P("region", None, None),
        P("region", None, None),
        P("region", None),
        P("region"),
    )
    out_specs = P("region", "member", None)
    return jax.shard_map(
        per_device, mesh=mesh, in_specs=in_specs, out_specs=out_specs, check_vma=False
    )
```

```python
import functools

import jax
import jax.numpy as jnp
from jax import lax
from jax.experimental import pallas as pl
from jax.experimental.pallas import tpu as pltpu
from jax.sharding import PartitionSpec as P

MESH = pl.DeviceIdType.MESH
ROWS = 64
PIECE = (16, 256)
TILE_BYTES = 24 << 20


def left_right(where):
    east, north = where[0:1], where[1:2]
    norm = east * east + north * north
    high = norm.astype(jnp.bfloat16).astype(jnp.float32)
    middle = (norm - high).astype(jnp.bfloat16).astype(jnp.float32)
    low = norm - high - middle
    row = lax.broadcasted_iota(jnp.int32, (16, where.shape[1]), 0)

    def stack(entries):
        out = jnp.zeros(row.shape, jnp.float32)
        for k, entry in enumerate(entries):
            out = jnp.where(row == k, entry, out)
        return out.astype(jnp.bfloat16)

    return (
        stack([east, north, high, middle, low, 1.0, 1.0, 1.0]),
        stack([-2.0 * east, -2.0 * north, 1.0, 1.0, 1.0, high, middle, low]),
    )


def gaspari_cohn(square):
    square = jnp.maximum(square, 2.0**-10)
    inverse = lax.rsqrt(square)
    z = square * inverse
    far = jnp.maximum(2.0 - z, 0.0)
    near = jnp.maximum(1.0 - z, 0.0)
    far = far * far
    near = near * near
    near = near + near
    both = square + z
    total = (far * far) * (both + (z - 0.5)) + (near * near) * (2.0 - both)
    return (total * (inverse * (1.0 / 12.0))).astype(jnp.bfloat16)


def kernel(
    regions, groups, levels,
    slots_ref, many_ref, ens_ref, inc_ref, where_ref,
    out_ref,
    place_out, place_in, rows_out, rows_in, inc_out, inc_in, weights, field, tiles, diag_tiles,
    square, diag_part, diag_in, pair_part, pair_in, home_out, home_in,
    place_send, place_recv, rows_send, rows_recv, inc_send, inc_recv, home_send, home_recv,
    half_send, half_recv, diag_send, diag_recv, pair_send, pair_recv,
    tile_send, tile_recv, own_send, own_recv,
):
    blocks, rows, points = ens_ref.shape
    members = rows // levels
    share = levels // groups
    me = lax.axis_index("region")
    my_group = lax.axis_index("member")

    core = lax.rem(my_group, 2)
    partner = my_group + 1 - 2 * core

    def region_at(step):
        out, bit = jnp.int32(0), 1
        while bit < regions:
            mine, other = lax.rem(lax.div(me, bit), 2), lax.rem(lax.div(jnp.int32(step), bit), 2)
            out = out + bit * (mine + other - 2 * mine * other)
            bit *= 2
        return out

    def to_region(src, dst, send, recv, d, at=None):
        return pltpu.make_async_remote_copy(
            src_ref=src.at[d], dst_ref=dst.at[d] if at is None else dst.at[d, at],
            send_sem=send.at[d], recv_sem=recv.at[d],
            device_id=(region_at(d), my_group), device_id_type=MESH,
        )

    def to_partner(ref, send, recv, *at):
        return pltpu.make_async_remote_copy(
            src_ref=ref.at[at], dst_ref=ref.at[at],
            send_sem=send.at[at[0]], recv_sem=recv.at[at[0]],
            device_id=(me, partner), device_id_type=MESH,
        )

    def to_group(src, dst, send, recv, d):
        other = lax.rem(my_group + d, groups)
        return pltpu.make_async_remote_copy(
            src_ref=src.at[other], dst_ref=dst.at[d], send_sem=send.at[d], recv_sem=recv.at[d],
            device_id=(me, other), device_id_type=MESH,
        )

    barrier = pltpu.get_barrier_semaphore()

    @pl.loop(1, regions)
    def _(d):
        pl.semaphore_signal(
            barrier, inc=1, device_id=(region_at(d), my_group), device_id_type=MESH
        )

    @pl.loop(1, groups)
    def _(d):
        pl.semaphore_signal(
            barrier, inc=1, device_id=(me, lax.rem(my_group + d, groups)), device_id_type=MESH
        )

    place_out[...] = jnp.zeros_like(place_out)
    for d in range(regions):
        slot = slots_ref[region_at(d)]
        places, sent = (place_in, rows_in) if d == 0 else (place_out, rows_out)
        places[d, 0:2] = where_ref[slot].astype(jnp.float32)
        sent[d] = ens_ref[slot]
        if d == 0:
            inc_in[0] = inc_ref[slot]
        else:
            inc_out[d] = inc_ref[slot, core]
    pl.semaphore_wait(barrier, regions + groups - 2)

    @pl.loop(1, regions)
    def _(d):
        to_region(place_out, place_in, place_send, place_recv, d).start()

    @pl.loop(1, regions)
    def _(d):
        to_region(inc_out, inc_in, inc_send, inc_recv, d, core).start()

    @pl.loop(1, regions)
    def _(d):
        to_region(rows_out, rows_in, rows_send, rows_recv, d).start()

    def weigh(member_rows, factor):
        factor = factor.astype(jnp.float32).reshape(levels, points)
        return jnp.concatenate(
            [
                (member_rows[m * levels : (m + 1) * levels].astype(jnp.float32) * factor).astype(
                    jnp.bfloat16
                )
                for m in range(members)
            ],
            0,
        )

    def over_members(member_rows, results):
        total = None
        for m in range(members):
            cut = slice(m * levels, (m + 1) * levels)
            term = member_rows[cut].astype(jnp.float32) * results[cut]
            total = term if total is None else total + term
        return total

    def make_tile(out, index, left_where, right_where):
        left, _ = left_right(left_where)
        _, right = left_right(right_where)
        square[...] = lax.dot_general(
            left, right, (((0,), (0,)), ((), ())), preferred_element_type=jnp.float32
        )
        tall, wide = min(ROWS, points), min(PIECE[1], points)

        @pl.loop(0, points // tall)
        def _(step):
            for row in range(0, tall, PIECE[0]):
                down = pl.ds(pl.multiple_of(step * tall + row, PIECE[0]), PIECE[0])
                for column in range(0, points, wide):
                    cut = (down, slice(column, column + wide))
                    out[(index, *cut)] = gaspari_cohn(square[cut])

    @pl.loop(0, blocks // 2)
    def _(k):
        b = 2 * k + core
        where = where_ref[b].astype(jnp.float32)
        make_tile(diag_tiles, b, where, where)
        to_partner(diag_tiles, own_send, own_recv, b).start()

    @pl.loop(1, regions)
    def _(d):
        to_region(inc_out, inc_in, inc_send, inc_recv, d, core).wait()
        to_partner(inc_in, half_send, half_recv, d, core).start()

    @pl.loop(0, blocks // 2)
    def _(k):
        to_partner(diag_tiles, own_send, own_recv, 2 * k + core).wait_send()
        to_partner(diag_tiles, own_send, own_recv, 2 * k + 1 - core).wait_recv()

    @pl.loop(0, blocks)
    def _(b):
        member_rows = ens_ref[b]
        results = jnp.dot(
            weigh(member_rows, inc_ref[b]), diag_tiles[b], preferred_element_type=jnp.float32
        )
        total = over_members(member_rows, results)
        for g in range(groups):
            diag_part[g, b] = total[g * share : (g + 1) * share]

    @pl.loop(1, groups)
    def _(d):
        to_group(diag_part, diag_in, diag_send, diag_recv, d).start()

    @pl.loop(1, regions)
    def _(d):
        to_region(place_out, place_in, place_send, place_recv, d).wait()

    keep = tiles.shape[0] > 1

    def half_of_pairs(which, do):
        @pl.loop(1, regions)
        def _(v):
            before = lax.div(v * (v - 1), 2)
            start = lax.rem(before + which, 2)

            @pl.loop(0, lax.div(v - start + 1, 2))
            def _(k):
                u = start + 2 * k
                do(u, v, before + u)

    def tile_away(u, v, index):
        make_tile(tiles, index, place_in[u], place_in[v])
        to_partner(tiles, tile_send, tile_recv, index).start()

    if keep:
        half_of_pairs(core, tile_away)

    @pl.loop(1, regions)
    def _(d):
        to_partner(inc_in, half_send, half_recv, d, core).wait_send()
        to_partner(inc_in, half_send, half_recv, d, 1 - core).wait_recv()

    field[...] = jnp.zeros_like(field)
    weights[0] = weigh(rows_in[0], inc_in[0])

    if keep:
        half_of_pairs(core, lambda u, v, i: to_partner(tiles, tile_send, tile_recv, i).wait_send())
        half_of_pairs(
            1 - core, lambda u, v, i: to_partner(tiles, tile_send, tile_recv, i).wait_recv()
        )

    @pl.loop(1, regions)
    def _(v):
        to_region(rows_out, rows_in, rows_send, rows_recv, v).wait()
        weights[v] = weigh(rows_in[v], inc_in[v])
        second = region_at(v)

        @pl.loop(0, v)
        def _(u):
            first = region_at(u)
            times = many_ref[first * regions + second]
            index = lax.div(v * (v - 1), 2) + u if keep else 0
            if not keep:
                make_tile(tiles, 0, place_in[u], place_in[v])
            field[u] += times * lax.dot_general(
                weights[v], tiles[index], (((1,), (1,)), ((), ())),
                preferred_element_type=jnp.float32,
            )
            field[v] += times * jnp.dot(
                weights[u], tiles[index], preferred_element_type=jnp.float32
            )

    @pl.loop(0, regions)
    def _(d):
        total = over_members(rows_in[d], field[d]).astype(pair_part.dtype)
        for g in range(groups):
            pair_part[g, d] = total[g * share : (g + 1) * share]

    @pl.loop(1, groups)
    def _(d):
        to_group(pair_part, pair_in, pair_send, pair_recv, d).start()

    @pl.loop(1, groups)
    def _(d):
        to_group(diag_part, diag_in, diag_send, diag_recv, d).wait()

    @pl.loop(1, groups)
    def _(d):
        to_group(pair_part, pair_in, pair_send, pair_recv, d).wait()

    for d in range(regions):
        total = pair_part[my_group, d].astype(jnp.float32)
        for g in range(1, groups):
            total = total + pair_in[g, d].astype(jnp.float32)
        (home_in if d == 0 else home_out)[d] = total.astype(home_in.dtype)

    @pl.loop(1, regions)
    def _(d):
        to_region(home_out, home_in, home_send, home_recv, d).start()

    @pl.loop(0, blocks)
    def _(b):
        total = diag_part[my_group, b]
        for g in range(1, groups):
            total = total + diag_in[g, b]
        out_ref[b] = total

    @pl.loop(1, regions)
    def _(d):
        to_region(home_out, home_in, home_send, home_recv, d).wait()

    @pl.loop(0, blocks)
    def _(b):
        total = out_ref[b]
        for d in range(regions):
            here = jnp.where(slots_ref[region_at(d)] == b, 1.0, 0.0)
            total = total + here * home_in[d].astype(jnp.float32)
        out_ref[b] = total


def per_device(ensemble, increment, coords, sent_slots, pair_list, pair_count):
    blocks, members, levels, points = ensemble.shape
    regions, groups = lax.axis_size("region"), lax.axis_size("member")
    share = levels // groups
    rows = members * levels
    live = jnp.arange(pair_list.shape[0], dtype=jnp.int32) < pair_count[0]
    low = jnp.min(pair_list, axis=1)
    high = jnp.max(pair_list, axis=1)
    home = jnp.arange(regions, dtype=jnp.int32)
    first, second = home[:, None, None], home[None, :, None]
    hit = (jnp.minimum(first, second) == low) & (jnp.maximum(first, second) == high) & live
    many = jnp.sum(hit.astype(jnp.float32), axis=2).reshape(regions * regions)
    pairs = regions * (regions - 1) // 2
    tile_total = pairs if pairs * points * points * 2 <= TILE_BYTES else 1
    part_kind = jnp.bfloat16 if share % 16 == 0 else jnp.float32
    vmem, smem = pl.BlockSpec(memory_space=pltpu.VMEM), pl.BlockSpec(memory_space=pltpu.SMEM)
    half = levels // 2
    region_dma = pltpu.SemaphoreType.DMA((regions,))
    group_dma = pltpu.SemaphoreType.DMA((groups,))
    f32, bf16 = jnp.float32, jnp.bfloat16
    summed = pl.pallas_call(
        functools.partial(kernel, regions, groups, levels),
        out_shape=jax.ShapeDtypeStruct((blocks, share, points), f32),
        in_specs=[smem, smem, vmem, vmem, vmem],
        out_specs=vmem,
        scratch_shapes=[
            pltpu.VMEM((regions, 8, points), f32),
            pltpu.VMEM((regions, 8, points), f32),
            pltpu.VMEM((regions, rows, points), bf16),
            pltpu.VMEM((regions, rows, points), bf16),
            pltpu.VMEM((regions, half, points), bf16),
            pltpu.VMEM((regions, 2, half, points), bf16),
            pltpu.VMEM((regions, rows, points), bf16),
            pltpu.VMEM((regions, rows, points), f32),
            pltpu.VMEM((tile_total, points, points), bf16),
            pltpu.VMEM((blocks, points, points), bf16),
            pltpu.VMEM((points, points), f32),
            pltpu.VMEM((groups, blocks, share, points), f32),
            pltpu.VMEM((groups, blocks, share, points), f32),
            pltpu.VMEM((groups, regions, share, points), part_kind),
            pltpu.VMEM((groups, regions, share, points), part_kind),
            pltpu.VMEM((regions, share, points), part_kind),
            pltpu.VMEM((regions, share, points), part_kind),
        ]
        + [region_dma] * 10 + [group_dma] * 4
        + [pltpu.SemaphoreType.DMA((tile_total,))] * 2
        + [pltpu.SemaphoreType.DMA((blocks,))] * 2,
        compiler_params=pltpu.CompilerParams(
            collective_id=0, has_side_effects=True, vmem_limit_bytes=56 << 20
        ),
    )(
        sent_slots[0, :, 0],
        many,
        ensemble.reshape(blocks, rows, points),
        increment.reshape(blocks, 2, half, points),
        coords,
    )
    return summed / (members * groups - 1)


def solution(mesh):
    in_specs = (
        P("region", "member", None, None),
        P("region", None, None),
        P("region", None, None),
        P("region", None, None),
        P("region", None),
        P("region"),
    )
    out_specs = P("region", "member", None)
    return jax.shard_map(
        per_device, mesh=mesh, in_specs=in_specs, out_specs=out_specs, check_vma=False
    )
```

```python
import functools

import jax
import jax.numpy as jnp
from jax import lax
from jax.experimental import pallas as pl
from jax.experimental.pallas import tpu as pltpu
from jax.sharding import PartitionSpec as P

MESH = pl.DeviceIdType.MESH
ROWS = 64
PIECE = (16, 256)
TILE_BYTES = 24 << 20


def left_right(where):
    east, north = where[0:1], where[1:2]
    norm = east * east + north * north
    high = norm.astype(jnp.bfloat16).astype(jnp.float32)
    middle = (norm - high).astype(jnp.bfloat16).astype(jnp.float32)
    low = norm - high - middle
    row = lax.broadcasted_iota(jnp.int32, (16, where.shape[1]), 0)

    def stack(entries):
        out = jnp.zeros(row.shape, jnp.float32)
        for k, entry in enumerate(entries):
            out = jnp.where(row == k, entry, out)
        return out.astype(jnp.bfloat16)

    return (
        stack([east, north, high, middle, low, 1.0, 1.0, 1.0]),
        stack([-2.0 * east, -2.0 * north, 1.0, 1.0, 1.0, high, middle, low]),
    )


def gaspari_cohn(square):
    square = jnp.maximum(square, 2.0**-10)
    inverse = lax.rsqrt(square)
    z = square * inverse
    far = jnp.maximum(2.0 - z, 0.0)
    near = jnp.maximum(1.0 - z, 0.0)
    far = far * far
    near = near * near
    near = near + near
    both = square + z
    total = (far * far) * (both + (z - 0.5)) + (near * near) * (2.0 - both)
    return (total * (inverse * (1.0 / 12.0))).astype(jnp.bfloat16)


def kernel(
    regions, groups, levels,
    slots_ref, count_ref, list_ref, ens_ref, inc_ref, where_ref,
    out_ref,
    place_out, place_in, rows_out, rows_in, inc_out, inc_in, weights, field, tiles, diag_tiles,
    square, diag_part, diag_in, pair_part, pair_in, home_out, home_in,
    place_send, place_recv, rows_send, rows_recv, inc_send, inc_recv, home_send, home_recv,
    half_send, half_recv, diag_send, diag_recv, pair_send, pair_recv,
    tile_send, tile_recv, own_send, own_recv,
):
    blocks, rows, points = ens_ref.shape
    members = rows // levels
    share = levels // groups
    me = lax.axis_index("region")
    my_group = lax.axis_index("member")

    core = lax.rem(my_group, 2)
    partner = my_group + 1 - 2 * core

    def region_at(step):
        out, bit = jnp.int32(0), 1
        while bit < regions:
            mine, other = lax.rem(lax.div(me, bit), 2), lax.rem(lax.div(jnp.int32(step), bit), 2)
            out = out + bit * (mine + other - 2 * mine * other)
            bit *= 2
        return out

    def to_region(src, dst, send, recv, d, at=None):
        return pltpu.make_async_remote_copy(
            src_ref=src.at[d], dst_ref=dst.at[d] if at is None else dst.at[d, at],
            send_sem=send.at[d], recv_sem=recv.at[d],
            device_id=(region_at(d), my_group), device_id_type=MESH,
        )

    def to_partner(ref, send, recv, *at):
        return pltpu.make_async_remote_copy(
            src_ref=ref.at[at], dst_ref=ref.at[at],
            send_sem=send.at[at[0]], recv_sem=recv.at[at[0]],
            device_id=(me, partner), device_id_type=MESH,
        )

    def to_group(src, dst, send, recv, d):
        other = lax.rem(my_group + d, groups)
        return pltpu.make_async_remote_copy(
            src_ref=src.at[other], dst_ref=dst.at[d], send_sem=send.at[d], recv_sem=recv.at[d],
            device_id=(me, other), device_id_type=MESH,
        )

    barrier = pltpu.get_barrier_semaphore()

    @pl.loop(1, regions)
    def _(d):
        pl.semaphore_signal(
            barrier, inc=1, device_id=(region_at(d), my_group), device_id_type=MESH
        )

    @pl.loop(1, groups)
    def _(d):
        pl.semaphore_signal(
            barrier, inc=1, device_id=(me, lax.rem(my_group + d, groups)), device_id_type=MESH
        )

    place_out[...] = jnp.zeros_like(place_out)
    for d in range(regions):
        slot = slots_ref[0, region_at(d), 0]
        places, sent = (place_in, rows_in) if d == 0 else (place_out, rows_out)
        places[d, 0:2] = where_ref[slot].astype(jnp.float32)
        sent[d] = ens_ref[slot]
        if d == 0:
            inc_in[0] = inc_ref[slot]
        else:
            inc_out[d] = inc_ref[slot, core]
    pl.semaphore_wait(barrier, regions + groups - 2)

    @pl.loop(1, regions)
    def _(d):
        to_region(place_out, place_in, place_send, place_recv, d).start()

    @pl.loop(1, regions)
    def _(d):
        to_region(inc_out, inc_in, inc_send, inc_recv, d, core).start()

    stages = [range(regions // 2, 3 * regions // 4), range(1, regions // 2)]
    later = [
        range(3 * regions // 4, 7 * regions // 8), range(7 * regions // 8, regions)
    ] if regions % 8 == 0 else [range(3 * regions // 4, regions), range(0)]

    def send_rows(steps):
        @pl.loop(steps.start, steps.stop)
        def _(d):
            to_region(rows_out, rows_in, rows_send, rows_recv, d).start()

    for steps in stages:
        send_rows(steps)

    def weigh(member_rows, factor):
        factor = factor.astype(jnp.float32).reshape(levels, points)
        return jnp.concatenate(
            [
                (member_rows[m * levels : (m + 1) * levels].astype(jnp.float32) * factor).astype(
                    jnp.bfloat16
                )
                for m in range(members)
            ],
            0,
        )

    def over_members(member_rows, results):
        total = None
        for m in range(members):
            cut = slice(m * levels, (m + 1) * levels)
            term = member_rows[cut].astype(jnp.float32) * results[cut]
            total = term if total is None else total + term
        return total

    def squares(left_where, right_where):
        left, _ = left_right(left_where)
        _, right = left_right(right_where)
        square[...] = lax.dot_general(
            left, right, (((0,), (0,)), ((), ())), preferred_element_type=jnp.float32
        )

    def fill(size, parts):
        tall, wide = min(ROWS, size), min(PIECE[1], size)

        @pl.loop(0, size // tall)
        def _(step):
            for row in range(0, tall, PIECE[0]):
                down = pl.multiple_of(step * tall + row, PIECE[0])
                for out, at, top, side in parts:
                    for column in range(0, size, wide):
                        out[(*at, pl.ds(down, PIECE[0]), slice(column, column + wide))] = gaspari_cohn(
                            square[
                                pl.ds(pl.multiple_of(down + top, PIECE[0]), PIECE[0]),
                                side + column : side + column + wide,
                            ]
                        )

    def make_tile(out, index, left_where, right_where):
        squares(left_where, right_where)
        fill(points, [(out, (index,), 0, 0)])

    half = points // 2

    @pl.loop(0, blocks // 2)
    def _(k):
        b = 2 * k + core
        where = where_ref[b].astype(jnp.float32)
        squares(where, where)
        fill(
            half,
            [
                (diag_tiles, (b, 0), 0, 0),
                (diag_tiles, (b, 1), 0, half),
                (diag_tiles, (b, 2), half, half),
            ],
        )
        to_partner(diag_tiles, own_send, own_recv, b).start()

    send_rows(later[0])

    @pl.loop(1, regions)
    def _(d):
        to_region(inc_out, inc_in, inc_send, inc_recv, d, core).wait()
        to_partner(inc_in, half_send, half_recv, d, core).start()

    @pl.loop(0, blocks // 2)
    def _(k):
        to_partner(diag_tiles, own_send, own_recv, 2 * k + core).wait_send()
        to_partner(diag_tiles, own_send, own_recv, 2 * k + 1 - core).wait_recv()

    @pl.loop(0, blocks)
    def _(b):
        member_rows = ens_ref[b]
        weighted = weigh(member_rows, inc_ref[b])
        first, second = weighted[:, :half], weighted[:, half:]
        corner = diag_tiles[b, 1]
        results = jnp.concatenate(
            [
                jnp.dot(first, diag_tiles[b, 0], preferred_element_type=jnp.float32)
                + lax.dot_general(
                    second, corner, (((1,), (1,)), ((), ())), preferred_element_type=jnp.float32
                ),
                jnp.dot(first, corner, preferred_element_type=jnp.float32)
                + jnp.dot(second, diag_tiles[b, 2], preferred_element_type=jnp.float32),
            ],
            1,
        )
        total = over_members(member_rows, results)
        for g in range(groups):
            diag_part[g, b] = total[g * share : (g + 1) * share]

    @pl.loop(1, groups)
    def _(d):
        to_group(diag_part, diag_in, diag_send, diag_recv, d).start()

    send_rows(later[1])

    @pl.loop(1, regions)
    def _(d):
        to_region(place_out, place_in, place_send, place_recv, d).wait()

    keep = tiles.shape[0] > 1

    def half_of_pairs(which, do):
        @pl.loop(1, regions)
        def _(v):
            before = lax.div(v * (v - 1), 2)
            start = lax.rem(before + which, 2)

            @pl.loop(0, lax.div(v - start + 1, 2))
            def _(k):
                u = start + 2 * k
                do(u, v, before + u)

    def tile_away(u, v, index):
        make_tile(tiles, index, place_in[u], place_in[v])
        to_partner(tiles, tile_send, tile_recv, index).start()

    if keep:
        half_of_pairs(core, tile_away)

    @pl.loop(1, regions)
    def _(d):
        to_partner(inc_in, half_send, half_recv, d, core).wait_send()
        to_partner(inc_in, half_send, half_recv, d, 1 - core).wait_recv()

    one_end, other_end = list_ref[:, 0:1], list_ref[:, 1:2]
    alive = jnp.where(
        lax.broadcasted_iota(jnp.int32, one_end.shape, 0) < count_ref[0], 1.0, 0.0
    )
    field[...] = jnp.zeros_like(field)
    weights[0] = weigh(rows_in[0], inc_in[0])

    if keep:
        half_of_pairs(core, lambda u, v, i: to_partner(tiles, tile_send, tile_recv, i).wait_send())
        half_of_pairs(
            1 - core, lambda u, v, i: to_partner(tiles, tile_send, tile_recv, i).wait_recv()
        )

    @pl.loop(1, regions)
    def _(v):
        to_region(rows_out, rows_in, rows_send, rows_recv, v).wait()
        weights[v] = weigh(rows_in[v], inc_in[v])
        second = region_at(v)

        @pl.loop(0, v)
        def _(u):
            first = region_at(u)
            listed = ((one_end == first) & (other_end == second)) | (
                (one_end == second) & (other_end == first)
            )
            times = jnp.sum(
                jnp.where(listed, alive, 0.0), axis=0, keepdims=True
            )
            index = lax.div(v * (v - 1), 2) + u if keep else 0
            if not keep:
                make_tile(tiles, 0, place_in[u], place_in[v])
            field[u] += times * lax.dot_general(
                weights[v], tiles[index], (((1,), (1,)), ((), ())),
                preferred_element_type=jnp.float32,
            )
            field[v] += times * jnp.dot(
                weights[u], tiles[index], preferred_element_type=jnp.float32
            )

    @pl.loop(0, regions)
    def _(d):
        total = over_members(rows_in[d], field[d]).astype(pair_part.dtype)
        for g in range(groups):
            pair_part[g, d] = total[g * share : (g + 1) * share]

    @pl.loop(1, groups)
    def _(d):
        to_group(pair_part, pair_in, pair_send, pair_recv, d).start()

    @pl.loop(1, groups)
    def _(d):
        to_group(diag_part, diag_in, diag_send, diag_recv, d).wait()

    @pl.loop(1, groups)
    def _(d):
        to_group(pair_part, pair_in, pair_send, pair_recv, d).wait()

    for d in reversed(range(regions)):
        total = pair_part[my_group, d].astype(jnp.float32)
        for g in range(1, groups):
            total = total + pair_in[g, d].astype(jnp.float32)
        (home_in if d == 0 else home_out)[d] = total.astype(home_in.dtype)
        if d > 0:
            to_region(home_out, home_in, home_send, home_recv, d).start()

    @pl.loop(0, blocks)
    def _(b):
        total = diag_part[my_group, b]
        for g in range(1, groups):
            total = total + diag_in[g, b]
        out_ref[b] = total

    @pl.loop(1, regions)
    def _(d):
        to_region(home_out, home_in, home_send, home_recv, d).wait()

    @pl.loop(0, blocks)
    def _(b):
        total = out_ref[b]
        for d in range(regions):
            here = jnp.where(slots_ref[0, region_at(d), 0] == b, 1.0, 0.0)
            total = total + here * home_in[d].astype(jnp.float32)
        out_ref[b] = total


def per_device(ensemble, increment, coords, sent_slots, pair_list, pair_count):
    blocks, members, levels, points = ensemble.shape
    regions, groups = lax.axis_size("region"), lax.axis_size("member")
    share = levels // groups
    rows = members * levels
    pairs = regions * (regions - 1) // 2
    tile_total = pairs if pairs * points * points * 2 <= TILE_BYTES else 1
    part_kind = jnp.bfloat16 if share % 16 == 0 else jnp.float32
    vmem, smem = pl.BlockSpec(memory_space=pltpu.VMEM), pl.BlockSpec(memory_space=pltpu.SMEM)
    half = levels // 2
    region_dma = pltpu.SemaphoreType.DMA((regions,))
    group_dma = pltpu.SemaphoreType.DMA((groups,))
    f32, bf16 = jnp.float32, jnp.bfloat16
    summed = pl.pallas_call(
        functools.partial(kernel, regions, groups, levels),
        out_shape=jax.ShapeDtypeStruct((blocks, share, points), f32),
        in_specs=[smem, smem, vmem, vmem, vmem, vmem],
        out_specs=vmem,
        scratch_shapes=[
            pltpu.VMEM((regions, 8, points), f32),
            pltpu.VMEM((regions, 8, points), f32),
            pltpu.VMEM((regions, rows, points), bf16),
            pltpu.VMEM((regions, rows, points), bf16),
            pltpu.VMEM((regions, half, points), bf16),
            pltpu.VMEM((regions, 2, half, points), bf16),
            pltpu.VMEM((regions, rows, points), bf16),
            pltpu.VMEM((regions, rows, points), f32),
            pltpu.VMEM((tile_total, points, points), bf16),
            pltpu.VMEM((blocks, 3, points // 2, points // 2), bf16),
            pltpu.VMEM((points, points), f32),
            pltpu.VMEM((groups, blocks, share, points), f32),
            pltpu.VMEM((groups, blocks, share, points), f32),
            pltpu.VMEM((groups, regions, share, points), part_kind),
            pltpu.VMEM((groups, regions, share, points), part_kind),
            pltpu.VMEM((regions, share, points), part_kind),
            pltpu.VMEM((regions, share, points), part_kind),
        ]
        + [region_dma] * 10 + [group_dma] * 4
        + [pltpu.SemaphoreType.DMA((tile_total,))] * 2
        + [pltpu.SemaphoreType.DMA((blocks,))] * 2,
        compiler_params=pltpu.CompilerParams(
            collective_id=0, has_side_effects=True, vmem_limit_bytes=56 << 20
        ),
    )(
        sent_slots,
        pair_count,
        pair_list,
        ensemble.reshape(blocks, rows, points),
        increment.reshape(blocks, 2, half, points),
        coords,
    )
    return summed / (members * groups - 1)


def solution(mesh):
    in_specs = (
        P("region", "member", None, None),
        P("region", None, None),
        P("region", None, None),
        P("region", None, None),
        P("region", None),
        P("region"),
    )
    out_specs = P("region", "member", None)
    return jax.shard_map(
        per_device, mesh=mesh, in_specs=in_specs, out_specs=out_specs, check_vma=False
    )
```

```python
import functools

import jax
import jax.numpy as jnp
from jax import lax
from jax.experimental import pallas as pl
from jax.experimental.pallas import tpu as pltpu
from jax.sharding import PartitionSpec as P

MESH = pl.DeviceIdType.MESH
ROWS = 64
PIECE = (16, 256)
TILE_BYTES = 24 << 20


def left_right(where):
    east, north = where[0:1], where[1:2]
    norm = east * east + north * north
    high = norm.astype(jnp.bfloat16).astype(jnp.float32)
    middle = (norm - high).astype(jnp.bfloat16).astype(jnp.float32)
    low = norm - high - middle
    row = lax.broadcasted_iota(jnp.int32, (16, where.shape[1]), 0)

    def stack(entries):
        out = jnp.zeros(row.shape, jnp.float32)
        for k, entry in enumerate(entries):
            out = jnp.where(row == k, entry, out)
        return out.astype(jnp.bfloat16)

    return (
        stack([east, north, high, middle, low, 1.0, 1.0, 1.0]),
        stack([-2.0 * east, -2.0 * north, 1.0, 1.0, 1.0, high, middle, low]),
    )


def gaspari_cohn(square, scale=1.0 / 12.0):
    square = jnp.maximum(square, 2.0**-10)
    inverse = lax.rsqrt(square)
    z = square * inverse
    far = jnp.maximum(2.0 - z, 0.0)
    near = jnp.maximum(1.0 - z, 0.0)
    far = far * far
    near = near * near
    near = near + near
    both = square + z
    total = (far * far) * (both + (z - 0.5)) + (near * near) * (2.0 - both)
    return (total * (inverse * scale)).astype(jnp.bfloat16)


def kernel(
    regions, groups, levels,
    slots_ref, many_ref, ens_ref, inc_ref, where_ref,
    out_ref,
    place_out, place_in, rows_out, rows_in, inc_out, inc_in, weights, field, tiles, diag_tiles,
    square, diag_part, diag_in, pair_part, pair_in, home_out, home_in,
    place_send, place_recv, rows_send, rows_recv, inc_send, inc_recv, home_send, home_recv,
    half_send, half_recv, diag_send, diag_recv, pair_send, pair_recv,
    tile_send, tile_recv, own_send, own_recv,
):
    blocks, rows, points = ens_ref.shape
    members = rows // levels
    share = levels // groups
    me = lax.axis_index("region")
    my_group = lax.axis_index("member")

    core = lax.rem(my_group, 2)
    partner = my_group + 1 - 2 * core

    def region_at(step):
        out, bit = jnp.int32(0), 1
        while bit < regions:
            mine, other = lax.rem(lax.div(me, bit), 2), lax.rem(lax.div(jnp.int32(step), bit), 2)
            out = out + bit * (mine + other - 2 * mine * other)
            bit *= 2
        return out

    def to_region(src, dst, send, recv, d, at=None):
        return pltpu.make_async_remote_copy(
            src_ref=src.at[d], dst_ref=dst.at[d] if at is None else dst.at[d, at],
            send_sem=send.at[d], recv_sem=recv.at[d],
            device_id=(region_at(d), my_group), device_id_type=MESH,
        )

    def to_partner(ref, send, recv, *at):
        return pltpu.make_async_remote_copy(
            src_ref=ref.at[at], dst_ref=ref.at[at],
            send_sem=send.at[at[0]], recv_sem=recv.at[at[0]],
            device_id=(me, partner), device_id_type=MESH,
        )

    def to_group(src, dst, send, recv, d):
        other = lax.rem(my_group + d, groups)
        return pltpu.make_async_remote_copy(
            src_ref=src.at[other], dst_ref=dst.at[d], send_sem=send.at[d], recv_sem=recv.at[d],
            device_id=(me, other), device_id_type=MESH,
        )

    barrier = pltpu.get_barrier_semaphore()

    @pl.loop(1, regions)
    def _(d):
        pl.semaphore_signal(
            barrier, inc=1, device_id=(region_at(d), my_group), device_id_type=MESH
        )

    @pl.loop(1, groups)
    def _(d):
        pl.semaphore_signal(
            barrier, inc=1, device_id=(me, lax.rem(my_group + d, groups)), device_id_type=MESH
        )

    place_out[...] = jnp.zeros_like(place_out)
    for d in range(regions):
        slot = slots_ref[region_at(d)]
        places, sent = (place_in, rows_in) if d == 0 else (place_out, rows_out)
        places[d, 0:2] = where_ref[slot].astype(jnp.float32)
        sent[d] = ens_ref[slot]
        if d == 0:
            inc_in[0] = inc_ref[slot]
        else:
            inc_out[d] = inc_ref[slot, core]
    pl.semaphore_wait(barrier, regions + groups - 2)

    @pl.loop(1, regions)
    def _(d):
        to_region(place_out, place_in, place_send, place_recv, d).start()

    @pl.loop(1, regions)
    def _(d):
        to_region(inc_out, inc_in, inc_send, inc_recv, d, core).start()

    def send_rows(steps):
        @pl.loop(steps.start, steps.stop)
        def _(d):
            to_region(rows_out, rows_in, rows_send, rows_recv, d).start()

    send_rows(range(regions // 2, regions))
    send_rows(range(1, regions // 2))

    def weigh(member_rows, factor):
        factor = factor.astype(jnp.float32).reshape(levels, points)
        return jnp.concatenate(
            [
                (member_rows[m * levels : (m + 1) * levels].astype(jnp.float32) * factor).astype(
                    jnp.bfloat16
                )
                for m in range(members)
            ],
            0,
        )

    def over_members(member_rows, results):
        total = None
        for m in range(members):
            cut = slice(m * levels, (m + 1) * levels)
            term = member_rows[cut].astype(jnp.float32) * results[cut]
            total = term if total is None else total + term
        return total

    def squares(left_where, right_where):
        left, _ = left_right(left_where)
        _, right = left_right(right_where)
        square[...] = lax.dot_general(
            left, right, (((0,), (0,)), ((), ())), preferred_element_type=jnp.float32
        )

    def fill(size, parts, scale=1.0 / 12.0, unroll=False):
        tall, wide = min(ROWS, size), min(PIECE[1], size)

        def some_rows(step):
            for row in range(0, tall, PIECE[0]):
                down = step * tall + row
                if not unroll:
                    down = pl.multiple_of(down, PIECE[0])
                for out, at, top, side in parts:
                    for column in range(0, size, wide):
                        out[(*at, pl.ds(down, PIECE[0]), slice(column, column + wide))] = gaspari_cohn(
                            square[
                                pl.ds(down + top, PIECE[0]), side + column : side + column + wide
                            ],
                            scale,
                        )

        if unroll:
            for step in range(size // tall):
                some_rows(step)
        else:
            pl.loop(0, size // tall)(some_rows)

    def make_pair_tile(index, u, v, unroll):
        squares(place_in[u], place_in[v])
        times = many_ref[region_at(u) * regions + region_at(v)]
        fill(points, [(tiles, (index,), 0, 0)], times * (1.0 / 12.0), unroll)

    half = points // 2

    @pl.loop(0, blocks // 2)
    def _(k):
        b = 2 * k + core
        where = where_ref[b].astype(jnp.float32)
        squares(where, where)
        fill(
            half,
            [
                (diag_tiles, (b, 0), 0, 0),
                (diag_tiles, (b, 1), 0, half),
                (diag_tiles, (b, 2), half, half),
            ],
        )
        to_partner(diag_tiles, own_send, own_recv, b).start()

    @pl.loop(1, regions)
    def _(d):
        to_region(inc_out, inc_in, inc_send, inc_recv, d, core).wait()
        to_partner(inc_in, half_send, half_recv, d, core).start()

    @pl.loop(0, blocks // 2)
    def _(k):
        to_partner(diag_tiles, own_send, own_recv, 2 * k + core).wait_send()
        to_partner(diag_tiles, own_send, own_recv, 2 * k + 1 - core).wait_recv()

    def diag_product(b):
        member_rows = ens_ref[b]
        weighted = weigh(member_rows, inc_ref[b])
        first, second = weighted[:, :half], weighted[:, half:]
        corner = diag_tiles[b, 1]
        results = jnp.concatenate(
            [
                jnp.dot(first, diag_tiles[b, 0], preferred_element_type=jnp.float32)
                + lax.dot_general(
                    second, corner, (((1,), (1,)), ((), ())), preferred_element_type=jnp.float32
                ),
                jnp.dot(first, corner, preferred_element_type=jnp.float32)
                + jnp.dot(second, diag_tiles[b, 2], preferred_element_type=jnp.float32),
            ],
            1,
        )
        total = over_members(member_rows, results)
        for g in range(groups):
            diag_part[g, b] = total[g * share : (g + 1) * share]

    @pl.loop(1, regions)
    def _(d):
        to_region(place_out, place_in, place_send, place_recv, d).wait()

    keep = tiles.shape[0] > 1

    def half_of_pairs(which, do):
        @pl.loop(1, regions)
        def _(v):
            before = lax.div(v * (v - 1), 2)
            start = lax.rem(before + which, 2)

            @pl.loop(0, lax.div(v - start + 1, 2))
            def _(k):
                u = start + 2 * k
                do(u, v, before + u)

    def tile_away(u, v, index):
        make_pair_tile(index, u, v, True)
        diag_product(lax.div(index, 2))
        to_partner(tiles, tile_send, tile_recv, index).start()

    done = 0
    if keep:
        half_of_pairs(core, tile_away)
        done = tiles.shape[0] // 2
    pl.loop(done, blocks)(diag_product)

    @pl.loop(1, groups)
    def _(d):
        to_group(diag_part, diag_in, diag_send, diag_recv, d).start()

    @pl.loop(1, regions)
    def _(d):
        to_partner(inc_in, half_send, half_recv, d, core).wait_send()
        to_partner(inc_in, half_send, half_recv, d, 1 - core).wait_recv()

    field[...] = jnp.zeros_like(field)
    weights[0] = weigh(rows_in[0], inc_in[0])

    if keep:
        half_of_pairs(core, lambda u, v, i: to_partner(tiles, tile_send, tile_recv, i).wait_send())
        half_of_pairs(
            1 - core, lambda u, v, i: to_partner(tiles, tile_send, tile_recv, i).wait_recv()
        )

    @pl.loop(1, regions)
    def _(v):
        to_region(rows_out, rows_in, rows_send, rows_recv, v).wait()
        weights[v] = weigh(rows_in[v], inc_in[v])

        @pl.loop(0, v)
        def _(u):
            index = lax.div(v * (v - 1), 2) + u if keep else 0
            if not keep:
                make_pair_tile(0, u, v, False)
            field[u] += lax.dot_general(
                weights[v], tiles[index], (((1,), (1,)), ((), ())),
                preferred_element_type=jnp.float32,
            )
            field[v] += jnp.dot(weights[u], tiles[index], preferred_element_type=jnp.float32)

    @pl.loop(0, regions)
    def _(d):
        total = over_members(rows_in[d], field[d]).astype(pair_part.dtype)
        for g in range(groups):
            pair_part[g, d] = total[g * share : (g + 1) * share]

    @pl.loop(1, groups)
    def _(d):
        to_group(pair_part, pair_in, pair_send, pair_recv, d).start()

    @pl.loop(1, groups)
    def _(d):
        to_group(diag_part, diag_in, diag_send, diag_recv, d).wait()

    @pl.loop(1, groups)
    def _(d):
        to_group(pair_part, pair_in, pair_send, pair_recv, d).wait()

    for d in reversed(range(regions)):
        total = pair_part[my_group, d].astype(jnp.float32)
        for g in range(1, groups):
            total = total + pair_in[g, d].astype(jnp.float32)
        (home_in if d == 0 else home_out)[d] = total.astype(home_in.dtype)
        if d > 0:
            to_region(home_out, home_in, home_send, home_recv, d).start()

    @pl.loop(0, blocks)
    def _(b):
        total = diag_part[my_group, b]
        for g in range(1, groups):
            total = total + diag_in[g, b]
        out_ref[b] = total

    @pl.loop(1, regions)
    def _(d):
        to_region(home_out, home_in, home_send, home_recv, d).wait()

    @pl.loop(0, blocks)
    def _(b):
        total = out_ref[b]
        for d in range(regions):
            here = jnp.where(slots_ref[region_at(d)] == b, 1.0, 0.0)
            total = total + here * home_in[d].astype(jnp.float32)
        out_ref[b] = total


def per_device(ensemble, increment, coords, sent_slots, pair_list, pair_count):
    blocks, members, levels, points = ensemble.shape
    regions, groups = lax.axis_size("region"), lax.axis_size("member")
    share = levels // groups
    rows = members * levels
    live = jnp.arange(pair_list.shape[0], dtype=jnp.int32) < pair_count[0]
    low, high = jnp.min(pair_list, axis=1), jnp.max(pair_list, axis=1)
    home = jnp.arange(regions, dtype=jnp.int32)
    first, second = home[:, None, None], home[None, :, None]
    hit = (jnp.minimum(first, second) == low) & (jnp.maximum(first, second) == high) & live
    many = jnp.sum(hit.astype(jnp.float32), axis=2).reshape(regions * regions)
    pairs = regions * (regions - 1) // 2
    tile_total = pairs if pairs * points * points * 2 <= TILE_BYTES and pairs <= 2 * blocks else 1
    part_kind = jnp.bfloat16 if share % 16 == 0 else jnp.float32
    vmem, smem = pl.BlockSpec(memory_space=pltpu.VMEM), pl.BlockSpec(memory_space=pltpu.SMEM)
    half = levels // 2
    region_dma = pltpu.SemaphoreType.DMA((regions,))
    group_dma = pltpu.SemaphoreType.DMA((groups,))
    f32, bf16 = jnp.float32, jnp.bfloat16
    summed = pl.pallas_call(
        functools.partial(kernel, regions, groups, levels),
        out_shape=jax.ShapeDtypeStruct((blocks, share, points), f32),
        in_specs=[smem, smem, vmem, vmem, vmem],
        out_specs=vmem,
        scratch_shapes=[
            pltpu.VMEM((regions, 8, points), f32),
            pltpu.VMEM((regions, 8, points), f32),
            pltpu.VMEM((regions, rows, points), bf16),
            pltpu.VMEM((regions, rows, points), bf16),
            pltpu.VMEM((regions, half, points), bf16),
            pltpu.VMEM((regions, 2, half, points), bf16),
            pltpu.VMEM((regions, rows, points), bf16),
            pltpu.VMEM((regions, rows, points), f32),
            pltpu.VMEM((tile_total, points, points), bf16),
            pltpu.VMEM((blocks, 3, points // 2, points // 2), bf16),
            pltpu.VMEM((points, points), f32),
            pltpu.VMEM((groups, blocks, share, points), f32),
            pltpu.VMEM((groups, blocks, share, points), f32),
            pltpu.VMEM((groups, regions, share, points), part_kind),
            pltpu.VMEM((groups, regions, share, points), part_kind),
            pltpu.VMEM((regions, share, points), part_kind),
            pltpu.VMEM((regions, share, points), part_kind),
        ]
        + [region_dma] * 10 + [group_dma] * 4
        + [pltpu.SemaphoreType.DMA((tile_total,))] * 2
        + [pltpu.SemaphoreType.DMA((blocks,))] * 2,
        compiler_params=pltpu.CompilerParams(
            collective_id=0, has_side_effects=True, vmem_limit_bytes=56 << 20
        ),
    )(
        sent_slots[0, :, 0],
        many,
        ensemble.reshape(blocks, rows, points),
        increment.reshape(blocks, 2, half, points),
        coords,
    )
    return summed / (members * groups - 1)


def solution(mesh):
    in_specs = (
        P("region", "member", None, None),
        P("region", None, None),
        P("region", None, None),
        P("region", None, None),
        P("region", None),
        P("region"),
    )
    out_specs = P("region", "member", None)
    return jax.shard_map(
        per_device, mesh=mesh, in_specs=in_specs, out_specs=out_specs, check_vma=False
    )
```

```python
import functools

import jax
import jax.numpy as jnp
from jax import lax
from jax.experimental import pallas as pl
from jax.experimental.pallas import tpu as pltpu
from jax.sharding import PartitionSpec as P

MESH = pl.DeviceIdType.MESH
ROWS = 64
PIECE = (16, 256)
TILE_BYTES = 24 << 20


def left_right(where):
    east, north = where[0:1], where[1:2]
    norm = east * east + north * north
    high = norm.astype(jnp.bfloat16).astype(jnp.float32)
    middle = (norm - high).astype(jnp.bfloat16).astype(jnp.float32)
    low = norm - high - middle
    row = lax.broadcasted_iota(jnp.int32, (16, where.shape[1]), 0)

    def stack(entries):
        out = jnp.zeros(row.shape, jnp.float32)
        for k, entry in enumerate(entries):
            out = jnp.where(row == k, entry, out)
        return out.astype(jnp.bfloat16)

    return (
        stack([east, north, high, middle, low, 1.0, 1.0, 1.0]),
        stack([-2.0 * east, -2.0 * north, 1.0, 1.0, 1.0, high, middle, low]),
    )


def gaspari_cohn(square, scale=1.0 / 12.0):
    square = jnp.maximum(square, 2.0**-10)
    inverse = lax.rsqrt(square)
    z = square * inverse
    far = jnp.maximum(2.0 - z, 0.0)
    near = jnp.maximum(1.0 - z, 0.0)
    far = far * far
    near = near * near
    near = near + near
    both = square + z
    total = (far * far) * (both + (z - 0.5)) + (near * near) * (2.0 - both)
    return (total * (inverse * scale)).astype(jnp.bfloat16)


def kernel(
    regions, groups, levels,
    slots_ref, many_ref, ens_ref, inc_ref, where_ref,
    out_ref,
    place_out, place_in, rows_out, rows_in, inc_out, inc_in, weights, field, tiles, diag_tiles,
    square, diag_part, diag_in, pair_part, pair_in, home_out, home_in,
    place_send, place_recv, rows_send, rows_recv, inc_send, inc_recv, home_send, home_recv,
    half_send, half_recv, diag_send, diag_recv, pair_send, pair_recv,
    tile_send, tile_recv, own_send, own_recv,
):
    blocks, rows, points = ens_ref.shape
    members = rows // levels
    share = levels // groups
    me = lax.axis_index("region")
    my_group = lax.axis_index("member")

    core = lax.rem(my_group, 2)
    partner = my_group + 1 - 2 * core

    def region_at(step):
        out, bit = jnp.int32(0), 1
        while bit < regions:
            mine, other = lax.rem(lax.div(me, bit), 2), lax.rem(lax.div(jnp.int32(step), bit), 2)
            out = out + bit * (mine + other - 2 * mine * other)
            bit *= 2
        return out

    def turn(t):
        t = jnp.int32(t)
        others = regions - 1
        some = lax.div(t + others, regions)
        near = regions // 2 - 1
        return some * (lax.rem(t - 1 + others + core * near, others) + 1)

    def to_region(src, dst, send, recv, d, at=None):
        return pltpu.make_async_remote_copy(
            src_ref=src.at[d], dst_ref=dst.at[d] if at is None else dst.at[d, at],
            send_sem=send.at[d], recv_sem=recv.at[d],
            device_id=(region_at(d), my_group), device_id_type=MESH,
        )

    def to_partner(ref, send, recv, *at):
        return pltpu.make_async_remote_copy(
            src_ref=ref.at[at], dst_ref=ref.at[at],
            send_sem=send.at[at[0]], recv_sem=recv.at[at[0]],
            device_id=(me, partner), device_id_type=MESH,
        )

    def to_group(src, dst, send, recv, d):
        other = lax.rem(my_group + d, groups)
        return pltpu.make_async_remote_copy(
            src_ref=src.at[other], dst_ref=dst.at[d], send_sem=send.at[d], recv_sem=recv.at[d],
            device_id=(me, other), device_id_type=MESH,
        )

    barrier = pltpu.get_barrier_semaphore()

    @pl.loop(1, regions)
    def _(d):
        pl.semaphore_signal(
            barrier, inc=1, device_id=(region_at(d), my_group), device_id_type=MESH
        )

    @pl.loop(1, groups)
    def _(d):
        pl.semaphore_signal(
            barrier, inc=1, device_id=(me, lax.rem(my_group + d, groups)), device_id_type=MESH
        )

    place_out[...] = jnp.zeros_like(place_out)
    for d in range(regions):
        slot = slots_ref[region_at(d)]
        places, sent = (place_in, rows_in) if d == 0 else (place_out, rows_out)
        places[d, 0:2] = where_ref[slot].astype(jnp.float32)
        sent[d] = ens_ref[slot]
        if d == 0:
            inc_in[0] = inc_ref[slot]
        else:
            inc_out[d] = inc_ref[slot, core]
    pl.semaphore_wait(barrier, regions + groups - 2)

    @pl.loop(1, regions)
    def _(d):
        to_region(place_out, place_in, place_send, place_recv, d).start()

    @pl.loop(1, regions)
    def _(d):
        to_region(inc_out, inc_in, inc_send, inc_recv, d, core).start()

    @pl.loop(1, regions)
    def _(t):
        to_region(rows_out, rows_in, rows_send, rows_recv, turn(t)).start()

    def weigh(member_rows, factor):
        factor = factor.astype(jnp.float32).reshape(levels, points)
        return jnp.concatenate(
            [
                (member_rows[m * levels : (m + 1) * levels].astype(jnp.float32) * factor).astype(
                    jnp.bfloat16
                )
                for m in range(members)
            ],
            0,
        )

    def over_members(member_rows, results):
        total = None
        for m in range(members):
            cut = slice(m * levels, (m + 1) * levels)
            term = member_rows[cut].astype(jnp.float32) * results[cut]
            total = term if total is None else total + term
        return total

    def squares(left_where, right_where):
        left, _ = left_right(left_where)
        _, right = left_right(right_where)
        square[...] = lax.dot_general(
            left, right, (((0,), (0,)), ((), ())), preferred_element_type=jnp.float32
        )

    def fill(size, parts, scale=1.0 / 12.0):
        tall, wide = min(ROWS, size), min(PIECE[1], size)

        def some_rows(step):
            for row in range(0, tall, PIECE[0]):
                down = pl.multiple_of(step * tall + row, PIECE[0])
                for out, at, top, side in parts:
                    for column in range(0, size, wide):
                        out[(*at, pl.ds(down, PIECE[0]), slice(column, column + wide))] = gaspari_cohn(
                            square[
                                pl.ds(pl.multiple_of(down + top, PIECE[0]), PIECE[0]), side + column : side + column + wide
                            ],
                            scale,
                        )

        pl.loop(0, size // tall)(some_rows)

    def make_pair_tile(index, u, v):
        squares(place_in[u], place_in[v])
        times = many_ref[region_at(u) * regions + region_at(v)]
        fill(points, [(tiles, (index,), 0, 0)], times * (1.0 / 12.0))

    half = points // 2

    @pl.loop(0, blocks // 2)
    def _(k):
        b = 2 * k + core
        where = where_ref[b].astype(jnp.float32)
        squares(where, where)
        fill(
            half,
            [
                (diag_tiles, (b, 0), 0, 0),
                (diag_tiles, (b, 1), 0, half),
                (diag_tiles, (b, 2), half, half),
            ],
        )
        to_partner(diag_tiles, own_send, own_recv, b).start()

    @pl.loop(1, regions)
    def _(d):
        to_region(inc_out, inc_in, inc_send, inc_recv, d, core).wait()
        to_partner(inc_in, half_send, half_recv, d, core).start()

    @pl.loop(0, blocks // 2)
    def _(k):
        to_partner(diag_tiles, own_send, own_recv, 2 * k + core).wait_send()
        to_partner(diag_tiles, own_send, own_recv, 2 * k + 1 - core).wait_recv()

    @pl.loop(0, blocks)
    def _(b):
        member_rows = ens_ref[b]
        weighted = weigh(member_rows, inc_ref[b])
        first, second = weighted[:, :half], weighted[:, half:]
        corner = diag_tiles[b, 1]
        results = jnp.concatenate(
            [
                jnp.dot(first, diag_tiles[b, 0], preferred_element_type=jnp.float32)
                + lax.dot_general(
                    second, corner, (((1,), (1,)), ((), ())), preferred_element_type=jnp.float32
                ),
                jnp.dot(first, corner, preferred_element_type=jnp.float32)
                + jnp.dot(second, diag_tiles[b, 2], preferred_element_type=jnp.float32),
            ],
            1,
        )
        total = over_members(member_rows, results)
        for g in range(groups):
            diag_part[g, b] = total[g * share : (g + 1) * share]

    @pl.loop(1, groups)
    def _(d):
        to_group(diag_part, diag_in, diag_send, diag_recv, d).start()

    @pl.loop(1, regions)
    def _(d):
        to_region(place_out, place_in, place_send, place_recv, d).wait()

    keep = tiles.shape[0] > 1

    def half_of_pairs(which, do):
        @pl.loop(1, regions)
        def _(v):
            before = lax.div(v * (v - 1), 2)
            start = lax.rem(before + which, 2)

            @pl.loop(0, lax.div(v - start + 1, 2))
            def _(k):
                u = start + 2 * k
                do(u, v, before + u)

    def tile_away(u, v, index):
        make_pair_tile(index, u, v)
        to_partner(tiles, tile_send, tile_recv, index).start()

    if keep:
        half_of_pairs(core, tile_away)

    @pl.loop(1, regions)
    def _(d):
        to_partner(inc_in, half_send, half_recv, d, core).wait_send()
        to_partner(inc_in, half_send, half_recv, d, 1 - core).wait_recv()

    field[...] = jnp.zeros_like(field)
    weights[0] = weigh(rows_in[0], inc_in[0])

    if keep:
        half_of_pairs(core, lambda u, v, i: to_partner(tiles, tile_send, tile_recv, i).wait_send())
        half_of_pairs(
            1 - core, lambda u, v, i: to_partner(tiles, tile_send, tile_recv, i).wait_recv()
        )

    @pl.loop(1, regions)
    def _(t):
        late = turn(t)
        to_region(rows_out, rows_in, rows_send, rows_recv, late).wait()
        weights[late] = weigh(rows_in[late], inc_in[late])

        @pl.loop(0, t)
        def _(before):
            early = turn(before)
            up = lax.div(late - early + regions, regions)
            v = up * late + (1 - up) * early
            u = late + early - v
            index = lax.div(v * (v - 1), 2) + u if keep else 0
            if not keep:
                make_pair_tile(0, u, v)
            field[u] += lax.dot_general(
                weights[v], tiles[index], (((1,), (1,)), ((), ())),
                preferred_element_type=jnp.float32,
            )
            field[v] += jnp.dot(weights[u], tiles[index], preferred_element_type=jnp.float32)

    @pl.loop(0, regions)
    def _(d):
        total = over_members(rows_in[d], field[d]).astype(pair_part.dtype)
        for g in range(groups):
            pair_part[g, d] = total[g * share : (g + 1) * share]

    @pl.loop(1, groups)
    def _(d):
        to_group(pair_part, pair_in, pair_send, pair_recv, d).start()

    @pl.loop(1, groups)
    def _(d):
        to_group(diag_part, diag_in, diag_send, diag_recv, d).wait()

    @pl.loop(1, groups)
    def _(d):
        to_group(pair_part, pair_in, pair_send, pair_recv, d).wait()

    for d in reversed(range(regions)):
        total = pair_part[my_group, d].astype(jnp.float32)
        for g in range(1, groups):
            total = total + pair_in[g, d].astype(jnp.float32)
        (home_in if d == 0 else home_out)[d] = total.astype(home_in.dtype)
        if d > 0:
            to_region(home_out, home_in, home_send, home_recv, d).start()

    @pl.loop(0, blocks)
    def _(b):
        total = diag_part[my_group, b]
        for g in range(1, groups):
            total = total + diag_in[g, b]
        out_ref[b] = total

    @pl.loop(1, regions)
    def _(d):
        to_region(home_out, home_in, home_send, home_recv, d).wait()

    @pl.loop(0, blocks)
    def _(b):
        total = out_ref[b]
        for d in range(regions):
            here = jnp.where(slots_ref[region_at(d)] == b, 1.0, 0.0)
            total = total + here * home_in[d].astype(jnp.float32)
        out_ref[b] = total


def per_device(ensemble, increment, coords, sent_slots, pair_list, pair_count):
    blocks, members, levels, points = ensemble.shape
    regions, groups = lax.axis_size("region"), lax.axis_size("member")
    share = levels // groups
    rows = members * levels
    live = jnp.arange(pair_list.shape[0], dtype=jnp.int32) < pair_count[0]
    low, high = jnp.min(pair_list, axis=1), jnp.max(pair_list, axis=1)
    home = jnp.arange(regions, dtype=jnp.int32)
    first, second = home[:, None, None], home[None, :, None]
    hit = (jnp.minimum(first, second) == low) & (jnp.maximum(first, second) == high) & live
    many = jnp.sum(hit.astype(jnp.float32), axis=2).reshape(regions * regions)
    pairs = regions * (regions - 1) // 2
    tile_total = pairs if pairs * points * points * 2 <= TILE_BYTES and pairs <= 2 * blocks else 1
    part_kind = jnp.bfloat16 if share % 16 == 0 else jnp.float32
    vmem, smem = pl.BlockSpec(memory_space=pltpu.VMEM), pl.BlockSpec(memory_space=pltpu.SMEM)
    half = levels // 2
    region_dma = pltpu.SemaphoreType.DMA((regions,))
    group_dma = pltpu.SemaphoreType.DMA((groups,))
    f32, bf16 = jnp.float32, jnp.bfloat16
    summed = pl.pallas_call(
        functools.partial(kernel, regions, groups, levels),
        out_shape=jax.ShapeDtypeStruct((blocks, share, points), f32),
        in_specs=[smem, smem, vmem, vmem, vmem],
        out_specs=vmem,
        scratch_shapes=[
            pltpu.VMEM((regions, 8, points), f32),
            pltpu.VMEM((regions, 8, points), f32),
            pltpu.VMEM((regions, rows, points), bf16),
            pltpu.VMEM((regions, rows, points), bf16),
            pltpu.VMEM((regions, half, points), bf16),
            pltpu.VMEM((regions, 2, half, points), bf16),
            pltpu.VMEM((regions, rows, points), bf16),
            pltpu.VMEM((regions, rows, points), f32),
            pltpu.VMEM((tile_total, points, points), bf16),
            pltpu.VMEM((blocks, 3, points // 2, points // 2), bf16),
            pltpu.VMEM((points, points), f32),
            pltpu.VMEM((groups, blocks, share, points), f32),
            pltpu.VMEM((groups, blocks, share, points), f32),
            pltpu.VMEM((groups, regions, share, points), part_kind),
            pltpu.VMEM((groups, regions, share, points), part_kind),
            pltpu.VMEM((regions, share, points), part_kind),
            pltpu.VMEM((regions, share, points), part_kind),
        ]
        + [region_dma] * 10 + [group_dma] * 4
        + [pltpu.SemaphoreType.DMA((tile_total,))] * 2
        + [pltpu.SemaphoreType.DMA((blocks,))] * 2,
        compiler_params=pltpu.CompilerParams(
            collective_id=0, has_side_effects=True, vmem_limit_bytes=56 << 20
        ),
    )(
        sent_slots[0, :, 0],
        many,
        ensemble.reshape(blocks, rows, points),
        increment.reshape(blocks, 2, half, points),
        coords,
    )
    return summed / (members * groups - 1)


def solution(mesh):
    in_specs = (
        P("region", "member", None, None),
        P("region", None, None),
        P("region", None, None),
        P("region", None, None),
        P("region", None),
        P("region"),
    )
    out_specs = P("region", "member", None)
    return jax.shard_map(
        per_device, mesh=mesh, in_specs=in_specs, out_specs=out_specs, check_vma=False
    )
```

```python
import functools

import jax
import jax.numpy as jnp
from jax import lax
from jax.experimental import pallas as pl
from jax.experimental.pallas import tpu as pltpu
from jax.sharding import PartitionSpec as P

MESH = pl.DeviceIdType.MESH
ROWS = 64
PIECE = (16, 256)
TILE_BYTES = 24 << 20


def left_right(where):
    east, north = where[0:1], where[1:2]
    norm = east * east + north * north
    high = norm.astype(jnp.bfloat16).astype(jnp.float32)
    middle = (norm - high).astype(jnp.bfloat16).astype(jnp.float32)
    low = norm - high - middle
    row = lax.broadcasted_iota(jnp.int32, (16, where.shape[1]), 0)

    def stack(entries):
        out = jnp.zeros(row.shape, jnp.float32)
        for k, entry in enumerate(entries):
            out = jnp.where(row == k, entry, out)
        return out.astype(jnp.bfloat16)

    return (
        stack([east, north, high, middle, low, 1.0, 1.0, 1.0]),
        stack([-2.0 * east, -2.0 * north, 1.0, 1.0, 1.0, high, middle, low]),
    )


def gaspari_cohn(square, scale):
    square = jnp.maximum(square, 2.0**-10)
    inverse = lax.rsqrt(square)
    z = square * inverse
    far = jnp.maximum(2.0 - z, 0.0)
    near = jnp.maximum(1.0 - z, 0.0)
    far = far * far
    near = near * near
    near = near + near
    both = square + z
    total = (far * far) * (both + (z - 0.5)) + (near * near) * (2.0 - both)
    return (total * (inverse * scale)).astype(jnp.bfloat16)


def kernel(
    regions, groups, levels,
    slots_ref, many_ref, ens_ref, inc_ref, where_ref,
    out_ref,
    place_out, place_in, rows_out, rows_in, inc_out, inc_in, weights, field, tiles, diag_tiles,
    square, diag_part, diag_in, pair_part, pair_in, home_out, home_in,
    place_send, place_recv, rows_send, rows_recv, inc_send, inc_recv, home_send, home_recv,
    half_send, half_recv, diag_send, diag_recv, pair_send, pair_recv,
    tile_send, tile_recv, own_send, own_recv,
):
    blocks, rows, points = ens_ref.shape
    members = rows // levels
    share = levels // groups
    me = lax.axis_index("region")
    my_group = lax.axis_index("member")

    core = lax.rem(my_group, 2)
    partner = my_group + 1 - 2 * core

    def region_at(step):
        out, bit = jnp.int32(0), 1
        while bit < regions:
            mine, other = lax.rem(lax.div(me, bit), 2), lax.rem(lax.div(jnp.int32(step), bit), 2)
            out = out + bit * (mine + other - 2 * mine * other)
            bit *= 2
        return out

    def to_region(src, dst, send, recv, d, at=None):
        return pltpu.make_async_remote_copy(
            src_ref=src.at[d], dst_ref=dst.at[d] if at is None else dst.at[d, at],
            send_sem=send.at[d], recv_sem=recv.at[d],
            device_id=(region_at(d), my_group), device_id_type=MESH,
        )

    def to_partner(ref, send, recv, *at):
        return pltpu.make_async_remote_copy(
            src_ref=ref.at[at], dst_ref=ref.at[at],
            send_sem=send.at[at[0]], recv_sem=recv.at[at[0]],
            device_id=(me, partner), device_id_type=MESH,
        )

    def to_group(src, dst, send, recv, d):
        other = lax.rem(my_group + d, groups)
        return pltpu.make_async_remote_copy(
            src_ref=src.at[other], dst_ref=dst.at[d], send_sem=send.at[d], recv_sem=recv.at[d],
            device_id=(me, other), device_id_type=MESH,
        )

    barrier = pltpu.get_barrier_semaphore()

    @pl.loop(1, regions)
    def _(d):
        pl.semaphore_signal(
            barrier, inc=1, device_id=(region_at(d), my_group), device_id_type=MESH
        )

    @pl.loop(1, groups)
    def _(d):
        pl.semaphore_signal(
            barrier, inc=1, device_id=(me, lax.rem(my_group + d, groups)), device_id_type=MESH
        )

    place_out[...] = jnp.zeros_like(place_out)
    for d in range(regions):
        slot = slots_ref[region_at(d)]
        places, sent = (place_in, rows_in) if d == 0 else (place_out, rows_out)
        places[d, 0:2] = where_ref[slot].astype(jnp.float32)
        sent[d] = ens_ref[slot]
        if d == 0:
            inc_in[0] = inc_ref[slot]
        else:
            inc_out[d] = inc_ref[slot, core]
    pl.semaphore_wait(barrier, regions + groups - 2)

    @pl.loop(1, regions)
    def _(d):
        to_region(place_out, place_in, place_send, place_recv, d).start()

    @pl.loop(1, regions)
    def _(d):
        to_region(inc_out, inc_in, inc_send, inc_recv, d, core).start()

    @pl.loop(1, regions)
    def _(d):
        to_region(rows_out, rows_in, rows_send, rows_recv, d).start()

    def weigh(member_rows, factor):
        factor = factor.astype(jnp.float32).reshape(levels, points)
        return jnp.concatenate(
            [
                (member_rows[m * levels : (m + 1) * levels].astype(jnp.float32) * factor).astype(
                    jnp.bfloat16
                )
                for m in range(members)
            ],
            0,
        )

    def over_members(member_rows, results):
        total = None
        for m in range(members):
            cut = slice(m * levels, (m + 1) * levels)
            term = member_rows[cut].astype(jnp.float32) * results[cut]
            total = term if total is None else total + term
        return total

    def make_tile(out, index, left_where, right_where, times=1.0):
        left, _ = left_right(left_where)
        _, right = left_right(right_where)
        square[...] = lax.dot_general(
            left, right, (((0,), (0,)), ((), ())), preferred_element_type=jnp.float32
        )
        tall, wide = min(ROWS, points), min(PIECE[1], points)
        scale = times * (1.0 / 12.0)

        @pl.loop(0, points // tall)
        def _(step):
            for row in range(0, tall, PIECE[0]):
                down = pl.ds(pl.multiple_of(step * tall + row, PIECE[0]), PIECE[0])
                for column in range(0, points, wide):
                    cut = (down, slice(column, column + wide))
                    out[(index, *cut)] = gaspari_cohn(square[cut], scale)

    @pl.loop(0, blocks // 2)
    def _(k):
        b = 2 * k + core
        where = where_ref[b].astype(jnp.float32)
        make_tile(diag_tiles, b, where, where)
        to_partner(diag_tiles, own_send, own_recv, b).start()

    @pl.loop(1, regions)
    def _(d):
        to_region(inc_out, inc_in, inc_send, inc_recv, d, core).wait()
        to_partner(inc_in, half_send, half_recv, d, core).start()

    @pl.loop(0, blocks // 2)
    def _(k):
        to_partner(diag_tiles, own_send, own_recv, 2 * k + core).wait_send()
        to_partner(diag_tiles, own_send, own_recv, 2 * k + 1 - core).wait_recv()

    @pl.loop(0, blocks)
    def _(b):
        member_rows = ens_ref[b]
        results = jnp.dot(
            weigh(member_rows, inc_ref[b]), diag_tiles[b], preferred_element_type=jnp.float32
        )
        total = over_members(member_rows, results)
        for g in range(groups):
            diag_part[g, b] = total[g * share : (g + 1) * share]

    @pl.loop(1, groups)
    def _(d):
        to_group(diag_part, diag_in, diag_send, diag_recv, d).start()

    @pl.loop(1, regions)
    def _(d):
        to_region(place_out, place_in, place_send, place_recv, d).wait()

    keep = tiles.shape[0] > 1

    def half_of_pairs(which, do):
        @pl.loop(1, regions)
        def _(v):
            before = lax.div(v * (v - 1), 2)
            start = lax.rem(before + which, 2)

            @pl.loop(0, lax.div(v - start + 1, 2))
            def _(k):
                u = start + 2 * k
                do(u, v, before + u)

    def pair_tile(index, u, v):
        times = many_ref[region_at(u) * regions + region_at(v)]
        make_tile(tiles, index, place_in[u], place_in[v], times)

    def tile_away(u, v, index):
        pair_tile(index, u, v)
        to_partner(tiles, tile_send, tile_recv, index).start()

    if keep:
        half_of_pairs(core, tile_away)

    @pl.loop(1, regions)
    def _(d):
        to_partner(inc_in, half_send, half_recv, d, core).wait_send()
        to_partner(inc_in, half_send, half_recv, d, 1 - core).wait_recv()

    field[...] = jnp.zeros_like(field)
    weights[0] = weigh(rows_in[0], inc_in[0])

    if keep:
        half_of_pairs(core, lambda u, v, i: to_partner(tiles, tile_send, tile_recv, i).wait_send())
        half_of_pairs(
            1 - core, lambda u, v, i: to_partner(tiles, tile_send, tile_recv, i).wait_recv()
        )

    @pl.loop(1, regions)
    def _(v):
        to_region(rows_out, rows_in, rows_send, rows_recv, v).wait()
        weights[v] = weigh(rows_in[v], inc_in[v])

        @pl.loop(0, v)
        def _(u):
            index = lax.div(v * (v - 1), 2) + u if keep else 0
            if not keep:
                pair_tile(0, u, v)
            field[u] += lax.dot_general(
                weights[v], tiles[index], (((1,), (1,)), ((), ())),
                preferred_element_type=jnp.float32,
            )
            field[v] += jnp.dot(weights[u], tiles[index], preferred_element_type=jnp.float32)

    @pl.loop(0, regions)
    def _(d):
        total = over_members(rows_in[d], field[d]).astype(pair_part.dtype)
        for g in range(groups):
            pair_part[g, d] = total[g * share : (g + 1) * share]

    @pl.loop(1, groups)
    def _(d):
        to_group(pair_part, pair_in, pair_send, pair_recv, d).start()

    @pl.loop(1, groups)
    def _(d):
        to_group(diag_part, diag_in, diag_send, diag_recv, d).wait()

    @pl.loop(1, groups)
    def _(d):
        to_group(pair_part, pair_in, pair_send, pair_recv, d).wait()

    for d in reversed(range(regions)):
        total = pair_part[my_group, d].astype(jnp.float32)
        for g in range(1, groups):
            total = total + pair_in[g, d].astype(jnp.float32)
        (home_in if d == 0 else home_out)[d] = total.astype(home_in.dtype)
        if d > 0:
            to_region(home_out, home_in, home_send, home_recv, d).start()

    @pl.loop(0, blocks)
    def _(b):
        total = diag_part[my_group, b]
        for g in range(1, groups):
            total = total + diag_in[g, b]
        out_ref[b] = total

    @pl.loop(1, regions)
    def _(d):
        to_region(home_out, home_in, home_send, home_recv, d).wait()

    @pl.loop(0, blocks)
    def _(b):
        total = out_ref[b]
        for d in range(regions):
            here = jnp.where(slots_ref[region_at(d)] == b, 1.0, 0.0)
            total = total + here * home_in[d].astype(jnp.float32)
        out_ref[b] = total


def per_device(ensemble, increment, coords, sent_slots, pair_list, pair_count):
    blocks, members, levels, points = ensemble.shape
    regions, groups = lax.axis_size("region"), lax.axis_size("member")
    share = levels // groups
    rows = members * levels
    live = jnp.arange(pair_list.shape[0], dtype=jnp.int32) < pair_count[0]
    low = jnp.min(pair_list, axis=1)
    high = jnp.max(pair_list, axis=1)
    home = jnp.arange(regions, dtype=jnp.int32)
    first, second = home[:, None, None], home[None, :, None]
    hit = (jnp.minimum(first, second) == low) & (jnp.maximum(first, second) == high) & live
    many = jnp.sum(hit.astype(jnp.float32), axis=2).reshape(regions * regions)
    pairs = regions * (regions - 1) // 2
    tile_total = pairs if pairs * points * points * 2 <= TILE_BYTES else 1
    part_kind = jnp.bfloat16 if share % 16 == 0 else jnp.float32
    vmem, smem = pl.BlockSpec(memory_space=pltpu.VMEM), pl.BlockSpec(memory_space=pltpu.SMEM)
    half = levels // 2
    region_dma = pltpu.SemaphoreType.DMA((regions,))
    group_dma = pltpu.SemaphoreType.DMA((groups,))
    f32, bf16 = jnp.float32, jnp.bfloat16
    summed = pl.pallas_call(
        functools.partial(kernel, regions, groups, levels),
        out_shape=jax.ShapeDtypeStruct((blocks, share, points), f32),
        in_specs=[smem, smem, vmem, vmem, vmem],
        out_specs=vmem,
        scratch_shapes=[
            pltpu.VMEM((regions, 8, points), f32),
            pltpu.VMEM((regions, 8, points), f32),
            pltpu.VMEM((regions, rows, points), bf16),
            pltpu.VMEM((regions, rows, points), bf16),
            pltpu.VMEM((regions, half, points), bf16),
            pltpu.VMEM((regions, 2, half, points), bf16),
            pltpu.VMEM((regions, rows, points), bf16),
            pltpu.VMEM((regions, rows, points), f32),
            pltpu.VMEM((tile_total, points, points), bf16),
            pltpu.VMEM((blocks, points, points), bf16),
            pltpu.VMEM((points, points), f32),
            pltpu.VMEM((groups, blocks, share, points), f32),
            pltpu.VMEM((groups, blocks, share, points), f32),
            pltpu.VMEM((groups, regions, share, points), part_kind),
            pltpu.VMEM((groups, regions, share, points), part_kind),
            pltpu.VMEM((regions, share, points), part_kind),
            pltpu.VMEM((regions, share, points), part_kind),
        ]
        + [region_dma] * 10 + [group_dma] * 4
        + [pltpu.SemaphoreType.DMA((tile_total,))] * 2
        + [pltpu.SemaphoreType.DMA((blocks,))] * 2,
        compiler_params=pltpu.CompilerParams(
            collective_id=0, has_side_effects=True, vmem_limit_bytes=56 << 20
        ),
    )(
        sent_slots[0, :, 0],
        many,
        ensemble.reshape(blocks, rows, points),
        increment.reshape(blocks, 2, half, points),
        coords,
    )
    return summed / (members * groups - 1)


def solution(mesh):
    in_specs = (
        P("region", "member", None, None),
        P("region", None, None),
        P("region", None, None),
        P("region", None, None),
        P("region", None),
        P("region"),
    )
    out_specs = P("region", "member", None)
    return jax.shard_map(
        per_device, mesh=mesh, in_specs=in_specs, out_specs=out_specs, check_vma=False
    )
```

```python
import functools

import jax
import jax.numpy as jnp
from jax import lax
from jax.experimental import pallas as pl
from jax.experimental.pallas import tpu as pltpu
from jax.sharding import PartitionSpec as P

MESH = pl.DeviceIdType.MESH
ROWS = 128
PIECE = (16, 256)
TILE_BYTES = 24 << 20


def left_right(where):
    east, north = where[0:1], where[1:2]
    norm = east * east + north * north
    high = norm.astype(jnp.bfloat16).astype(jnp.float32)
    middle = (norm - high).astype(jnp.bfloat16).astype(jnp.float32)
    low = norm - high - middle
    row = lax.broadcasted_iota(jnp.int32, (16, where.shape[1]), 0)

    def stack(entries):
        out = jnp.zeros(row.shape, jnp.float32)
        for k, entry in enumerate(entries):
            out = jnp.where(row == k, entry, out)
        return out.astype(jnp.bfloat16)

    return (
        stack([east, north, high, middle, low, 1.0, 1.0, 1.0]),
        stack([-2.0 * east, -2.0 * north, 1.0, 1.0, 1.0, high, middle, low]),
    )


def gaspari_cohn(square, scale):
    square = jnp.maximum(square, 2.0**-10)
    inverse = lax.rsqrt(square)
    z = square * inverse
    far = jnp.maximum(2.0 - z, 0.0)
    near = jnp.maximum(1.0 - z, 0.0)
    far = far * far
    near = near * near
    near = near + near
    both = square + z
    total = (far * far) * (both + (z - 0.5)) + (near * near) * (2.0 - both)
    return (total * (inverse * scale)).astype(jnp.bfloat16)


def kernel(
    regions, groups, levels,
    slots_ref, many_ref, ens_ref, inc_ref, where_ref,
    out_ref,
    place_out, place_in, rows_out, rows_in, inc_out, inc_in, weights, field, tiles, diag_tiles,
    square, diag_part, diag_in, pair_part, pair_in, home_out, home_in,
    place_send, place_recv, rows_send, rows_recv, inc_send, inc_recv, home_send, home_recv,
    half_send, half_recv, diag_send, diag_recv, pair_send, pair_recv,
    tile_send, tile_recv, own_send, own_recv,
):
    blocks, rows, points = ens_ref.shape
    members = rows // levels
    share = levels // groups
    me = lax.axis_index("region")
    my_group = lax.axis_index("member")

    core = lax.rem(my_group, 2)
    partner = my_group + 1 - 2 * core

    def region_at(step):
        out, bit = jnp.int32(0), 1
        while bit < regions:
            mine, other = lax.rem(lax.div(me, bit), 2), lax.rem(lax.div(jnp.int32(step), bit), 2)
            out = out + bit * (mine + other - 2 * mine * other)
            bit *= 2
        return out

    def to_region(src, dst, send, recv, d, at=None):
        return pltpu.make_async_remote_copy(
            src_ref=src.at[d], dst_ref=dst.at[d] if at is None else dst.at[d, at],
            send_sem=send.at[d], recv_sem=recv.at[d],
            device_id=(region_at(d), my_group), device_id_type=MESH,
        )

    def to_partner(ref, send, recv, *at):
        return pltpu.make_async_remote_copy(
            src_ref=ref.at[at], dst_ref=ref.at[at],
            send_sem=send.at[at[0]], recv_sem=recv.at[at[0]],
            device_id=(me, partner), device_id_type=MESH,
        )

    def to_group(src, dst, send, recv, d):
        other = lax.rem(my_group + d, groups)
        return pltpu.make_async_remote_copy(
            src_ref=src.at[other], dst_ref=dst.at[d], send_sem=send.at[d], recv_sem=recv.at[d],
            device_id=(me, other), device_id_type=MESH,
        )

    barrier = pltpu.get_barrier_semaphore()

    @pl.loop(1, regions)
    def _(d):
        pl.semaphore_signal(
            barrier, inc=1, device_id=(region_at(d), my_group), device_id_type=MESH
        )

    @pl.loop(1, groups)
    def _(d):
        pl.semaphore_signal(
            barrier, inc=1, device_id=(me, lax.rem(my_group + d, groups)), device_id_type=MESH
        )

    place_out[...] = jnp.zeros_like(place_out)
    for d in range(regions):
        slot = slots_ref[region_at(d)]
        places, sent = (place_in, rows_in) if d == 0 else (place_out, rows_out)
        places[d, 0:2] = where_ref[slot].astype(jnp.float32)
        sent[d] = ens_ref[slot]
        if d == 0:
            inc_in[0] = inc_ref[slot]
        else:
            inc_out[d] = inc_ref[slot, core]
    pl.semaphore_wait(barrier, regions + groups - 2)

    @pl.loop(1, regions)
    def _(d):
        to_region(place_out, place_in, place_send, place_recv, d).start()

    @pl.loop(1, regions)
    def _(d):
        to_region(inc_out, inc_in, inc_send, inc_recv, d, core).start()

    @pl.loop(1, regions)
    def _(d):
        to_region(rows_out, rows_in, rows_send, rows_recv, d).start()

    def weigh(member_rows, factor):
        factor = factor.astype(jnp.float32).reshape(levels, points)
        return jnp.concatenate(
            [
                (member_rows[m * levels : (m + 1) * levels].astype(jnp.float32) * factor).astype(
                    jnp.bfloat16
                )
                for m in range(members)
            ],
            0,
        )

    def over_members(member_rows, results):
        total = None
        for m in range(members):
            cut = slice(m * levels, (m + 1) * levels)
            term = member_rows[cut].astype(jnp.float32) * results[cut]
            total = term if total is None else total + term
        return total

    def make_tile(out, index, left_where, right_where, times=1.0):
        left, _ = left_right(left_where)
        _, right = left_right(right_where)
        square[...] = lax.dot_general(
            left, right, (((0,), (0,)), ((), ())), preferred_element_type=jnp.float32
        )
        tall, wide = min(ROWS, points), min(PIECE[1], points)
        scale = times * (1.0 / 12.0)

        @pl.loop(0, points // tall)
        def _(step):
            for row in range(0, tall, PIECE[0]):
                down = pl.ds(pl.multiple_of(step * tall + row, PIECE[0]), PIECE[0])
                for column in range(0, points, wide):
                    cut = (down, slice(column, column + wide))
                    out[(index, *cut)] = gaspari_cohn(square[cut], scale)

    @pl.loop(0, blocks // 2)
    def _(k):
        b = 2 * k + core
        where = where_ref[b].astype(jnp.float32)
        make_tile(diag_tiles, b, where, where)
        to_partner(diag_tiles, own_send, own_recv, b).start()

    @pl.loop(1, regions)
    def _(d):
        to_region(inc_out, inc_in, inc_send, inc_recv, d, core).wait()
        to_partner(inc_in, half_send, half_recv, d, core).start()

    @pl.loop(0, blocks // 2)
    def _(k):
        to_partner(diag_tiles, own_send, own_recv, 2 * k + core).wait_send()
        to_partner(diag_tiles, own_send, own_recv, 2 * k + 1 - core).wait_recv()

    @pl.loop(0, blocks)
    def _(b):
        member_rows = ens_ref[b]
        results = jnp.dot(
            weigh(member_rows, inc_ref[b]), diag_tiles[b], preferred_element_type=jnp.float32
        )
        total = over_members(member_rows, results)
        for g in range(groups):
            diag_part[g, b] = total[g * share : (g + 1) * share]

    @pl.loop(1, groups)
    def _(d):
        to_group(diag_part, diag_in, diag_send, diag_recv, d).start()

    @pl.loop(1, regions)
    def _(d):
        to_region(place_out, place_in, place_send, place_recv, d).wait()

    keep = tiles.shape[0] > 1

    def half_of_pairs(which, do):
        @pl.loop(1, regions)
        def _(v):
            before = lax.div(v * (v - 1), 2)
            start = lax.rem(before + which, 2)

            @pl.loop(0, lax.div(v - start + 1, 2))
            def _(k):
                u = start + 2 * k
                do(u, v, before + u)

    def pair_tile(index, u, v):
        times = many_ref[region_at(u) * regions + region_at(v)]
        make_tile(tiles, index, place_in[u], place_in[v], times)

    def tile_away(u, v, index):
        pair_tile(index, u, v)
        to_partner(tiles, tile_send, tile_recv, index).start()

    if keep:
        half_of_pairs(core, tile_away)

    @pl.loop(1, regions)
    def _(d):
        to_partner(inc_in, half_send, half_recv, d, core).wait_send()
        to_partner(inc_in, half_send, half_recv, d, 1 - core).wait_recv()

    field[...] = jnp.zeros_like(field)
    weights[0] = weigh(rows_in[0], inc_in[0])

    if keep:
        half_of_pairs(core, lambda u, v, i: to_partner(tiles, tile_send, tile_recv, i).wait_send())
        half_of_pairs(
            1 - core, lambda u, v, i: to_partner(tiles, tile_send, tile_recv, i).wait_recv()
        )

    @pl.loop(1, regions)
    def _(v):
        to_region(rows_out, rows_in, rows_send, rows_recv, v).wait()
        weights[v] = weigh(rows_in[v], inc_in[v])

        @pl.loop(0, v)
        def _(u):
            index = lax.div(v * (v - 1), 2) + u if keep else 0
            if not keep:
                pair_tile(0, u, v)
            field[u] += lax.dot_general(
                weights[v], tiles[index], (((1,), (1,)), ((), ())),
                preferred_element_type=jnp.float32,
            )
            field[v] += jnp.dot(weights[u], tiles[index], preferred_element_type=jnp.float32)

    @pl.loop(0, regions)
    def _(d):
        total = over_members(rows_in[d], field[d]).astype(pair_part.dtype)
        for g in range(groups):
            pair_part[g, d] = total[g * share : (g + 1) * share]

    @pl.loop(1, groups)
    def _(d):
        to_group(pair_part, pair_in, pair_send, pair_recv, d).start()

    @pl.loop(1, groups)
    def _(d):
        to_group(diag_part, diag_in, diag_send, diag_recv, d).wait()

    @pl.loop(1, groups)
    def _(d):
        to_group(pair_part, pair_in, pair_send, pair_recv, d).wait()

    for d in reversed(range(regions)):
        total = pair_part[my_group, d].astype(jnp.float32)
        for g in range(1, groups):
            total = total + pair_in[g, d].astype(jnp.float32)
        (home_in if d == 0 else home_out)[d] = total.astype(home_in.dtype)
        if d > 0:
            to_region(home_out, home_in, home_send, home_recv, d).start()

    @pl.loop(0, blocks)
    def _(b):
        total = diag_part[my_group, b]
        for g in range(1, groups):
            total = total + diag_in[g, b]
        out_ref[b] = total

    @pl.loop(1, regions)
    def _(d):
        to_region(home_out, home_in, home_send, home_recv, d).wait()

    @pl.loop(0, blocks)
    def _(b):
        total = out_ref[b]
        for d in range(regions):
            here = jnp.where(slots_ref[region_at(d)] == b, 1.0, 0.0)
            total = total + here * home_in[d].astype(jnp.float32)
        out_ref[b] = total


def per_device(ensemble, increment, coords, sent_slots, pair_list, pair_count):
    blocks, members, levels, points = ensemble.shape
    regions, groups = lax.axis_size("region"), lax.axis_size("member")
    share = levels // groups
    rows = members * levels
    live = jnp.arange(pair_list.shape[0], dtype=jnp.int32) < pair_count[0]
    low = jnp.min(pair_list, axis=1)
    high = jnp.max(pair_list, axis=1)
    home = jnp.arange(regions, dtype=jnp.int32)
    first, second = home[:, None, None], home[None, :, None]
    hit = (jnp.minimum(first, second) == low) & (jnp.maximum(first, second) == high) & live
    many = jnp.sum(hit.astype(jnp.float32), axis=2).reshape(regions * regions)
    pairs = regions * (regions - 1) // 2
    tile_total = pairs if pairs * points * points * 2 <= TILE_BYTES else 1
    part_kind = jnp.bfloat16 if share % 16 == 0 else jnp.float32
    vmem, smem = pl.BlockSpec(memory_space=pltpu.VMEM), pl.BlockSpec(memory_space=pltpu.SMEM)
    half = levels // 2
    region_dma = pltpu.SemaphoreType.DMA((regions,))
    group_dma = pltpu.SemaphoreType.DMA((groups,))
    f32, bf16 = jnp.float32, jnp.bfloat16
    summed = pl.pallas_call(
        functools.partial(kernel, regions, groups, levels),
        out_shape=jax.ShapeDtypeStruct((blocks, share, points), f32),
        in_specs=[smem, smem, vmem, vmem, vmem],
        out_specs=vmem,
        scratch_shapes=[
            pltpu.VMEM((regions, 8, points), f32),
            pltpu.VMEM((regions, 8, points), f32),
            pltpu.VMEM((regions, rows, points), bf16),
            pltpu.VMEM((regions, rows, points), bf16),
            pltpu.VMEM((regions, half, points), bf16),
            pltpu.VMEM((regions, 2, half, points), bf16),
            pltpu.VMEM((regions, rows, points), bf16),
            pltpu.VMEM((regions, rows, points), f32),
            pltpu.VMEM((tile_total, points, points), bf16),
            pltpu.VMEM((blocks, points, points), bf16),
            pltpu.VMEM((points, points), f32),
            pltpu.VMEM((groups, blocks, share, points), f32),
            pltpu.VMEM((groups, blocks, share, points), f32),
            pltpu.VMEM((groups, regions, share, points), part_kind),
            pltpu.VMEM((groups, regions, share, points), part_kind),
            pltpu.VMEM((regions, share, points), part_kind),
            pltpu.VMEM((regions, share, points), part_kind),
        ]
        + [region_dma] * 10 + [group_dma] * 4
        + [pltpu.SemaphoreType.DMA((tile_total,))] * 2
        + [pltpu.SemaphoreType.DMA((blocks,))] * 2,
        compiler_params=pltpu.CompilerParams(
            collective_id=0, has_side_effects=True, vmem_limit_bytes=56 << 20
        ),
    )(
        sent_slots[0, :, 0],
        many,
        ensemble.reshape(blocks, rows, points),
        increment.reshape(blocks, 2, half, points),
        coords,
    )
    return summed / (members * groups - 1)


def solution(mesh):
    in_specs = (
        P("region", "member", None, None),
        P("region", None, None),
        P("region", None, None),
        P("region", None, None),
        P("region", None),
        P("region"),
    )
    out_specs = P("region", "member", None)
    return jax.shard_map(
        per_device, mesh=mesh, in_specs=in_specs, out_specs=out_specs, check_vma=False
    )
```
